256 devices in a mesh: seq: 64 (over x, z, core), head: 4 (over y).
Axes of the slice: x: 4, y: 4, z: 8, core: 2. Of those that a mesh axis runs over, the one named last changes fastest.
Arguments:
- queries: bfloat16 [128, 8192], P('seq', 'head'), may hold values from -8 to 8
- sys_cache: bfloat16 [4096, 2, 1024], P('seq', None, 'head'), may hold values from -8 to 8
- ctx_cache: bfloat16 [32768, 2, 1024], P('seq', None, 'head'), may hold values from -6 to 6
- block_context: int32 [128], P('seq'), may hold values from 0 to 15, as said below
- context_id: int32 [128], P('seq'), may hold values from 0 to 15
- suffix_cache: bfloat16 [128, 1024, 2, 1024], P('seq', None, None, 'head'), may hold values from -6 to 6
- suffix_lengths: int32 [128], P('seq'), may hold values from 1 to 1024, 81920 in all
- out_weight: bfloat16 [8192, 5120], P('head', 'seq'), may hold values from -0.0625 to 0.0625
Outputs:
- mixed: float32 [128, 5120], P('head', 'seq')
The draws below stay inside these ranges and needn't reach their ends.
Inputs may be any that keep to these rules, and one draw needn't show every extreme that they name: `block_context`: each of the 16 contexts is named by exactly 8 blocks.
All inputs are finite; a program needn't handle non-finite values. No bound on the sum of `suffix_lengths` on one device may be relied on, other than what follows from the above.
Results may differ from the reference program's by a relative error of at most 0.0065.
Values may be sent and summed in bfloat16 or wider, within the bound.
A program may use at most 128 MiB of HBM per device.

```python
import math
import jax
import jax.numpy as jnp
import numpy as np
from jax import lax

QH = 64
KVH = 8
HD = 128
DM = 5120
SUF = 1024
BLK = 256
CTXS = 16
REQUESTS = 128
SYS = 4096
NBLK = 128
CTX = 2048


def draw_queries(key, part):
    own_key = jax.random.fold_in(key, 3)
    values = 2.5 * jax.random.normal(own_key, (REQUESTS, QH * HD), dtype=jnp.float32)
    return jnp.clip(values, -8.0, 8.0).astype(jnp.bfloat16)


def draw_sys_cache(key, part):
    own_key = jax.random.fold_in(key, 5)
    values = jax.random.normal(own_key, (SYS, 2, KVH * HD), dtype=jnp.float32)
    return jnp.clip(values, -6.0, 6.0).astype(jnp.bfloat16)


def draw_block_context(key, part):
    own_key = jax.random.fold_in(key, 7)
    order = jax.random.permutation(own_key, NBLK).astype(jnp.int32)
    return (order // (NBLK // CTXS)).astype(jnp.int32)


def with_ends(entries, stream_key, least, top_value):
    spot = [jax.random.randint(jax.random.fold_in(stream_key, axis), (), 0, length) for axis, length in enumerate(entries.shape)]
    widest = entries.shape.index(max(entries.shape))
    next_to = spot[:widest] + [(spot[widest] + 1) % entries.shape[widest]] + spot[widest + 1:]
    return entries.at[tuple(spot)].set(least).at[tuple(next_to)].set(top_value)


def shard_levels(rng, shape, cuts, least, high):
    level = 1.0
    for dim, blocks in cuts:
        draws = jax.random.uniform(jax.random.fold_in(jax.random.fold_in(rng, 6), dim), (blocks,), jnp.float32, least / len(cuts), high / len(cuts))
        level = level * jnp.repeat(jnp.exp(draws), shape[dim] // blocks).reshape((-1,) + (1,) * (len(shape) - 1 - dim))
    return level


def cumulative_ranks(number_of, slope):
    weights = [(1 << 20) // math.isqrt(rank ** slope) + 1 for rank in range(1, number_of + 1)]
    spread = 1 + sum(weights) // (1 << 30)
    return np.cumsum(np.array([max(1, weight // spread) for weight in weights]))


def ranked(key, shape, amount, lean):
    table = cumulative_ranks(amount, lean)
    ticket = jax.random.randint(jax.random.fold_in(key, 1), shape, 0, int(table[amount - 1]))
    grade = jnp.searchsorted(jnp.asarray(table, jnp.int32), ticket, side="right")
    return jax.random.permutation(jax.random.fold_in(key, 2), amount)[grade].astype(jnp.int32)


def split_up(amount, total, most, lean):
    loads = [(1 << 20) // math.isqrt(grade ** lean) + 1 for grade in range(2, amount + 1)]
    rest, holding = total - most - (amount - 1), [1] * (amount - 1)
    while rest > 0:
        movable = [i for i in range(amount - 1) if holding[i] < most]
        whole, remaining = sum([loads[i] for i in movable]), rest
        for i in movable:
            extra = min(most - holding[i], max(1, remaining * loads[i] // whole), rest)
            holding[i] = holding[i] + extra
            rest = rest - extra
    return np.array([most] + holding)


def ragged(rng, count, total, bound, slope):
    if count == 2:
        one = jax.random.randint(rng, (), max(1, total - bound), min(bound, total - 1) + 1)
        return jnp.stack([one, total - one])
    sizes = jnp.asarray(split_up(count, total, bound, slope), jnp.int32)
    pairs = (count - 1) // 2
    giver, receiver = sizes[1:1 + 2 * pairs:2], sizes[2:2 + 2 * pairs:2]
    room = jnp.minimum(giver - 1, bound - receiver)
    shifted = jax.random.randint(jax.random.fold_in(rng, 1), (pairs,), 0, 1 << 20) % (room + 1)
    sizes = sizes.at[1:1 + 2 * pairs:2].set(giver - shifted).at[2:2 + 2 * pairs:2].set(receiver + shifted)
    return sizes[jax.random.permutation(jax.random.fold_in(rng, 2), count)]


def centred(key, extent, width, most, cuts=(), kind=jnp.bfloat16):
    values = jax.random.normal(key, extent, jnp.float32) * width
    if len(cuts) > 0:
        values = shard_levels(key, extent, cuts, -0.22, 0.18) * values
    return jnp.clip(values, min=-most, max=most).astype(kind)


def setup_inputs(seed: int = 0) -> dict:
    streams_of = jax.random.split(jax.random.key(seed), 9)
    return {
        "queries": draw_queries(jax.random.fold_in(streams_of[8], 71), 0),
        "sys_cache": draw_sys_cache(jax.random.fold_in(streams_of[8], 71), 0),
        "ctx_cache": centred(streams_of[2], (NBLK * BLK, 2, KVH * HD), 1.0, 6.0, ((0, 64), (2, 4))),
        "block_context": draw_block_context(jax.random.fold_in(streams_of[8], 71), 0),
        "context_id": with_ends(ranked(streams_of[4], (REQUESTS,), CTXS, 2), jax.random.fold_in(streams_of[4], 3), 0, CTXS - 1).astype(jnp.int32),
        "suffix_cache": centred(streams_of[5], (REQUESTS, SUF, 2, KVH * HD), 1.0, 6.0, ((0, 64), (3, 4))),
        "suffix_lengths": ragged(streams_of[6], REQUESTS, REQUESTS * SUF * 5 // 8, SUF, 2).astype(jnp.int32),
        "out_weight": centred(streams_of[7], (QH * HD, DM), (QH * HD) ** -0.5, 0.0625, ((0, 4), (1, 64))),
    }


def reference(queries, sys_cache, ctx_cache, block_context, context_id, suffix_cache, suffix_lengths, out_weight):
    group_size = QH // KVH
    score_scale = 1.0 / math.sqrt(HD)
    sys_keys = sys_cache[:, 0].astype(jnp.float32).reshape(SYS, KVH, HD)
    sys_values = sys_cache[:, 1].astype(jnp.float32).reshape(SYS, KVH, HD)
    ctx_keys = ctx_cache[:, 0].astype(jnp.float32).reshape(NBLK * BLK, KVH, HD)
    ctx_values = ctx_cache[:, 1].astype(jnp.float32).reshape(NBLK * BLK, KVH, HD)
    token_context = jnp.repeat(block_context, BLK)
    context_rows = jnp.argsort(token_context, stable=True).astype(jnp.int32).reshape(CTXS, CTX)
    block_size = math.gcd(REQUESTS, 4)

    def rounded_weights(scores, top):
        weights = jnp.exp(scores - top[..., None]).astype(jnp.bfloat16)
        return lax.optimization_barrier(weights).astype(jnp.float32)

    def attend(block_index):
        first_row = (block_index * block_size).astype(jnp.int32)
        query_block = lax.dynamic_slice_in_dim(queries, first_row, block_size, 0).astype(jnp.float32)
        query_block = query_block.reshape(block_size, KVH, group_size, HD)
        owned_context = lax.dynamic_slice_in_dim(context_id, first_row, block_size, 0)
        lengths_here = lax.dynamic_slice_in_dim(suffix_lengths, first_row, block_size, 0)
        suffix_block = lax.dynamic_slice_in_dim(suffix_cache, first_row, block_size, 0).astype(jnp.float32)
        suffix_keys = suffix_block[:, :, 0].reshape(block_size, SUF, KVH, HD)
        suffix_values = suffix_block[:, :, 1].reshape(block_size, SUF, KVH, HD)
        picked = context_rows[owned_context]
        picked_keys = ctx_keys[picked]
        picked_values = ctx_values[picked]
        system_scores = jnp.einsum('bgjd,tgd->bgjt', query_block, sys_keys) * score_scale
        context_scores = jnp.einsum('bgjd,btgd->bgjt', query_block, picked_keys) * score_scale
        suffix_scores = jnp.einsum('bgjd,btgd->bgjt', query_block, suffix_keys) * score_scale
        live = jnp.arange(SUF, dtype=jnp.int32)[None, :] < lengths_here[:, None]
        suffix_scores = jnp.where(live[:, None, None, :], suffix_scores, -jnp.inf)
        top = jnp.maximum(jnp.maximum(system_scores.max(-1), context_scores.max(-1)), suffix_scores.max(-1))
        system_weights = rounded_weights(system_scores, top)
        context_weights = rounded_weights(context_scores, top)
        suffix_weights = rounded_weights(suffix_scores, top)
        numerator = jnp.einsum('bgjt,tgd->bgjd', system_weights, sys_values)
        numerator = numerator + jnp.einsum('bgjt,btgd->bgjd', context_weights, picked_values)
        numerator = numerator + jnp.einsum('bgjt,btgd->bgjd', suffix_weights, suffix_values)
        totals = system_weights.sum(-1) + context_weights.sum(-1) + suffix_weights.sum(-1)
        attention = numerator / totals[..., None]
        return attention.reshape(block_size, QH * HD).astype(jnp.bfloat16)
    attention = lax.map(attend, jnp.arange(REQUESTS // block_size, dtype=jnp.int32)).reshape(REQUESTS, QH * HD)
    return jnp.dot(attention, out_weight, preferred_element_type=jnp.float32)
```

```python
import math

import jax
import jax.numpy as jnp
from jax import lax
from jax.experimental import pallas as pl
from jax.experimental.pallas import tpu as pltpu
from jax.sharding import PartitionSpec as P

HD = 128
NX, NZ, NC, NY = 4, 8, 2, 4
SLOTS = NZ * NC
GROUP = 8
ROWS = SLOTS * GROUP * 2
SYS_T, CTX_T, SUF_T = 64, 512, 1024
TOK = 2 * (SYS_T + CTX_T)
BLOCK = 256
COLS = 80
VROWS = HD + 16
SCALE = math.log2(math.e) / math.sqrt(HD)
LOW = -1e30
MASKED = -3e38
MESH = pl.DeviceIdType.MESH
F32, BF16 = jnp.float32, jnp.bfloat16
CHUNK = 256


def dot(a, b):
    return lax.dot_general(a, b, (((1,), (0,)), ((), ())), preferred_element_type=F32)


def dot_t(a, b):
    return lax.dot_general(a, b, (((1,), (1,)), ((), ())), preferred_element_type=F32)


def iota(shape, dim):
    return lax.broadcasted_iota(jnp.int32, shape, dim)


def kernel(
    cid_ref, len_ref, bc_ref, q_hbm, sys_hbm, ctx_hbm, suf_hbm, wt_hbm, out_ref,
    qown, qg, kvx, keys, vt, sufx, qbd, ssuf, nsuf, suf_s, sufml_s, suf_r, sufml_r, bc_s, bc_r, idbuf, idx,
    perm, pick, eye,
    rx_s, rxml_s, rx_r, rxml_r, rz_s, rzml_s, rz_r, rzml_r, az, ax, wt, ys, yr,
    loc, sib_s, sib_r, zq_s, zq_r, zi_s, zi_r, xq_s, xq_r, xi_s, xi_r, rx_ss, rx_rs, rxm_ss, rxm_rs,
    rz_ss, rz_rs, rzm_ss, rzm_rs, az_ss, az_rs, ax_ss, ax_rs, y_ss, y_rs,
):
    seq, y = lax.axis_index("seq"), lax.axis_index("head")
    x, z, c = lax.div(seq, SLOTS), lax.rem(lax.div(seq, NC), NZ), lax.rem(seq, NC)
    o = 1 - c
    slot = z * NC + c

    def device(xx, zz, cc, yy):
        return ((xx * NZ + zz) * NC + cc, yy)

    def remote(src, dst, send, recv, where):
        return pltpu.make_async_remote_copy(
            src_ref=src, dst_ref=dst, send_sem=send, recv_sem=recv, device_id=where, device_id_type=MESH
        )

    sibling = device(x, z, o, y)
    z_peers = [(lax.rem(z + k, NZ), lax.rem(c + d, NC)) for k in (4, 3, 5, 2, 6, 1, 7, 0) for d in (0, 1) if k + d > 0]
    z_own = [lax.rem(z + k, NZ) for k in (4, 3, 5, 2, 6, 1, 7)]
    x_peers = [lax.rem(x + k, NX) for k in (2, 1, 3)]
    y_peers = [(lax.rem(y + k, NY), lax.rem(c + d, NC)) for k in (2, 1, 3, 0) for d in (0, 1) if k + d > 0]

    own_128 = pl.ds(pl.multiple_of(c * HD, HD), HD)
    other_128 = pl.ds(pl.multiple_of(o * HD, HD), HD)
    own_w = pl.ds(pl.multiple_of(c * GROUP * HD, HD), GROUP * HD)
    other_w = pl.ds(pl.multiple_of(o * GROUP * HD, HD), GROUP * HD)
    copy_q = pltpu.make_async_copy(q_hbm.at[pl.ds(c * GROUP, GROUP)], qg.at[x, slot], loc.at[0])
    copy_ctx = pltpu.make_async_copy(ctx_hbm.at[:, :, own_128], kvx.at[pl.ds(2 * SYS_T, CTX_T)], loc.at[1])
    copy_sys = pltpu.make_async_copy(sys_hbm.at[:, :, own_128], kvx.at[pl.ds(0, SYS_T)], loc.at[2])
    copy_suf = pltpu.make_async_copy(suf_hbm, sufx, loc.at[3])
    copy_own = pltpu.make_async_copy(q_hbm, qown, loc.at[4])
    copy_wt = pltpu.make_async_copy(wt_hbm.at[:, own_w], wt.at[0], loc.at[5])
    for copy in (copy_q, copy_ctx, copy_sys, copy_own, copy_suf, copy_wt):
        copy.start()

    barrier = pltpu.get_barrier_semaphore()
    partners = [device(x, zz, cc, y) for zz, cc in z_peers]
    partners += [device(xx, z, c, y) for xx in x_peers]
    partners += [device(x, z, cc, yy) for yy, cc in y_peers[:-1]]
    for partner in partners:
        pl.semaphore_signal(barrier, inc=1, device_id=partner, device_id_type=MESH)

    lane = iota((1, HD), 1)
    idbuf[slot] = jnp.where(
        lax.div(lane, 16) == lax.rem(slot, 8),
        jnp.where(lax.rem(lane, 2) == 0, cid_ref[0], cid_ref[1]),
        0,
    )
    bc_s[0] = jnp.full((1, HD), bc_ref[0], jnp.int32)
    bc_s[1] = jnp.full((1, HD), bc_ref[1], jnp.int32)

    pl.semaphore_wait(barrier, len(partners))

    sends = []
    for zz, cc in z_peers:
        peer = zz * NC + cc
        copy = remote(
            q_hbm.at[pl.ds(cc * GROUP, GROUP)], qg.at[x, slot], zq_s.at[peer], zq_r.at[slot], device(x, zz, cc, y)
        )
        copy.start()
        sends.append(copy)
    for zz, cc in z_peers:
        peer = zz * NC + cc
        copy = remote(idbuf.at[slot], idbuf.at[slot], zi_s.at[peer], zi_r.at[slot], device(x, zz, cc, y))
        copy.start()
        sends.append(copy)

    swaps = [
        remote(sys_hbm.at[:, :, other_128], kvx.at[pl.ds(SYS_T, SYS_T)], sib_s.at[0], sib_r.at[0], sibling),
        remote(
            ctx_hbm.at[:, :, other_128], kvx.at[pl.ds(2 * SYS_T + CTX_T, CTX_T)], sib_s.at[1], sib_r.at[1], sibling
        ),
        remote(bc_s, bc_r, sib_s.at[2], sib_r.at[2], sibling),
        remote(wt_hbm.at[:, other_w], wt.at[1], sib_s.at[3], sib_r.at[3], sibling),
    ]
    for copy in swaps:
        copy.start()
        sends.append(copy)

    row, col = iota((256, 256), 0), iota((256, 256), 1)
    perm[...] = (col == jnp.where(row < HD, 2 * row, 2 * (row - HD) + 1)).astype(F32).astype(BF16)
    rest = lax.rem(row, 32)
    pick[...] = (col == lax.div(rest, 2) * 16 + lax.div(row, 32) * 2 + lax.rem(rest, 2)).astype(F32).astype(BF16)
    eye[...] = (iota((HD, HD), 0) == iota((HD, HD), 1)).astype(F32).astype(BF16)
    vt[pl.ds(HD, 16), :] = jnp.ones((16, TOK), BF16)
    flat = kvx.reshape(2 * TOK, HD)

    def take_apart(part, _):
        pairs = flat[pl.ds(pl.multiple_of(part * 256, 256), 256), :]
        both = dot(perm[...], pairs).astype(BF16)
        start = pl.multiple_of(part * HD, HD)
        keys[pl.ds(start, HD), :] = both[:HD]
        vt[pl.ds(0, HD), pl.ds(start, HD)] = dot_t(eye[...], both[HD:]).astype(BF16)
        return 0

    copy_ctx.wait()
    lax.fori_loop(1, 5, take_apart, 0)
    copy_sys.wait()
    swaps[0].wait_recv()
    swaps[1].wait_recv()
    lax.fori_loop(5, 9, take_apart, 0)
    take_apart(0, 0)

    copy_q.wait()
    for zz, cc in z_peers:
        peer = zz * NC + cc
        remote(q_hbm.at[pl.ds(0, GROUP)], qg.at[x, peer], zq_s.at[peer], zq_r.at[peer], sibling).wait_recv()
    for xx in x_peers:
        copy = remote(qg.at[x], qg.at[x], xq_s.at[xx], xq_r.at[x], device(xx, z, c, y))
        copy.start()
        sends.append(copy)
    for zz, cc in z_peers:
        peer = zz * NC + cc
        remote(idbuf.at[peer], idbuf.at[peer], zi_s.at[peer], zi_r.at[peer], sibling).wait_recv()
    idx[x, 0] = sum([idbuf[k] for k in range(1, 8)], idbuf[0])
    idx[x, 1] = sum([idbuf[k] for k in range(9, 16)], idbuf[8])
    for xx in x_peers:
        copy = remote(idx.at[x], idx.at[x], xi_s.at[xx], xi_r.at[x], device(xx, z, c, y))
        copy.start()
        sends.append(copy)
    swaps[2].wait_recv()

    def partial(xx):
        queries = qg.at[xx].reshape(ROWS, HD)[...]
        ids = jnp.concatenate([idx[xx, 0], idx[xx, 1]], axis=1)
        parts = []
        for b in range(5):
            start, size = (0, 2 * SYS_T) if b == 0 else (2 * SYS_T + (b - 1) * BLOCK, BLOCK)
            scores = dot_t(keys[pl.ds(start, size), :], queries)
            top = jnp.max(scores, axis=0, keepdims=True)
            weights = jnp.exp2(scores * SCALE - top * SCALE).astype(BF16)
            sums = dot(vt[:, pl.ds(start, size)], weights)
            if b > 0:
                if b <= 2:
                    ok = ids == bc_ref[b - 1]
                else:
                    theirs = bc_r[b - 3]
                    ok = ids == jnp.concatenate([theirs, theirs], axis=1)
                top = jnp.where(ok, top, LOW)
            parts.append((top, sums))
        largest = parts[0][0]
        for top, _ in parts[1:]:
            largest = jnp.maximum(largest, top)
        total = None
        for top, sums in parts:
            scaled = sums * jnp.exp2((top - largest) * SCALE)
            total = scaled if total is None else total + scaled
        return total[:HD], largest, total[HD : HD + 1]

    num_own, m_own, l_own = partial(x)
    rx_s[x] = num_own.astype(BF16)
    rxml_s[x, 0] = m_own
    rxml_s[x, 1] = l_own

    copy_own.wait()
    copy_suf.wait()
    qbd[...] = jnp.zeros((HD, 2 * HD), BF16)
    qrows = qown.reshape(32, HD)
    own_16, other_16 = pl.multiple_of(16 * c, 16), pl.multiple_of(16 * o, 16)
    qbd[pl.ds(own_16, 16), own_128] = qrows[pl.ds(own_16, 16), :]
    qbd[pl.ds(32 + own_16, 16), other_128] = qrows[pl.ds(other_16, 16), :]
    first = lax.rem(lane, 2) == 0
    place = lax.div(lane, 16)
    valid = (place == c) | (place == 2 + c)
    live = jnp.where(valid, jnp.where(first, 2 * len_ref[0], 2 * len_ref[1]), 0)
    suf_rows = sufx.reshape(2, 2 * SUF_T, 2 * HD)

    def suffix_scores(part, top):
        start = pl.multiple_of(part * CHUNK, CHUNK)
        spread = qbd[...]
        one = dot_t(suf_rows[0, pl.ds(start, CHUNK), :], spread)
        two = dot_t(suf_rows[1, pl.ds(start, CHUNK), :], spread)
        at = iota((CHUNK, HD), 0)
        at = jnp.where(lax.rem(at, 2) == 0, at + start, 1 << 20)
        scores = jnp.where(at < live, jnp.where(first, one, two), MASKED)
        ssuf[pl.ds(start, CHUNK), :] = scores
        return jnp.maximum(top, jnp.max(scores, axis=0, keepdims=True))

    m_suf = lax.fori_loop(0, 2 * SUF_T // CHUNK, suffix_scores, jnp.full((1, HD), LOW, F32))
    nsuf[...] = jnp.zeros((2, HD, 2 * HD), F32)

    def suffix_sums(part, total):
        start = pl.multiple_of(part * CHUNK, CHUNK)
        weights = jnp.exp2(ssuf[pl.ds(start, CHUNK), :] * SCALE - m_suf * SCALE)
        weights = weights.astype(BF16).astype(F32)
        turned = pltpu.roll(weights, 1, 0).T.astype(BF16)
        for i in range(2):
            nsuf[i] += dot(turned, suf_rows[i, pl.ds(start, CHUNK), :])
        return total + jnp.sum(weights, axis=0, keepdims=True)

    l_suf = lax.fori_loop(0, 2 * SUF_T // CHUNK, suffix_sums, jnp.zeros((1, HD), F32))
    even = lax.rem(iota((HD, HD), 0), 2) == 0
    suf_s[...] = pltpu.roll(jnp.where(even, nsuf[0, :, other_128], nsuf[1, :, other_128]).T, HD - 32, 1)
    sufml_s[0] = pltpu.roll(jnp.broadcast_to(m_suf, (8, HD)), HD - 32, 1)[:1]
    sufml_s[1] = pltpu.roll(jnp.broadcast_to(l_suf, (8, HD)), HD - 32, 1)[:1]
    to_sibling = [
        remote(suf_s, suf_r, sib_s.at[4], sib_r.at[4], sibling),
        remote(sufml_s, sufml_r, sib_s.at[5], sib_r.at[5], sibling),
    ]
    for copy in to_sibling:
        copy.start()
        sends.append(copy)
    n_suf = jnp.where(even, nsuf[0, :, own_128], nsuf[1, :, own_128]).T

    def other_x(step, _):
        xx = lax.rem(x + lax.div(step * (step + 1), 2), NX)
        remote(qg.at[x], qg.at[xx], xq_s.at[xx], xq_r.at[xx], sibling).wait_recv()
        remote(idx.at[x], idx.at[xx], xi_s.at[xx], xi_r.at[xx], sibling).wait_recv()
        num, m, l = partial(xx)
        rx_s[xx] = num.astype(BF16)
        rxml_s[xx, 0] = m
        rxml_s[xx, 1] = l
        where = device(xx, z, c, y)
        remote(rx_s.at[xx], rx_r.at[x], rx_ss.at[xx], rx_rs.at[x], where).start()
        remote(rxml_s.at[xx], rxml_r.at[x], rxm_ss.at[xx], rxm_rs.at[x], where).start()
        return 0

    lax.fori_loop(1, NX, other_x, 0)

    for copy in to_sibling:
        copy.wait_recv()
    mine = place == c
    shift = lax.rem(z, 4) * 32
    both_n = pltpu.roll(jnp.where(mine, n_suf, suf_r[...]), shift, 1)
    both_m = pltpu.roll(jnp.broadcast_to(jnp.where(mine, m_suf, sufml_r[0]), (8, HD)), shift, 1)[:1]
    both_l = pltpu.roll(jnp.broadcast_to(jnp.where(mine, l_suf, sufml_r[1]), (8, HD)), shift, 1)[:1]
    here = lax.div(iota((1, ROWS), 1), 32) == z
    suf_n = jnp.where(here, jnp.concatenate([both_n, both_n], axis=1), 0.0)
    suf_m = jnp.where(here, jnp.concatenate([both_m, both_m], axis=1), LOW)
    suf_l = jnp.where(here, jnp.concatenate([both_l, both_l], axis=1), 0.0)

    for xx in x_peers:
        remote(rx_s.at[xx], rx_r.at[xx], rx_ss.at[xx], rx_rs.at[xx], sibling).wait_recv()
        remote(rxml_s.at[xx], rxml_r.at[xx], rxm_ss.at[xx], rxm_rs.at[xx], sibling).wait_recv()
    tops = [rxml_s[x, 0], suf_m] + [rxml_r[xx, 0] for xx in x_peers]
    totals = [rxml_s[x, 1], suf_l] + [rxml_r[xx, 1] for xx in x_peers]
    largest = tops[0]
    for top in tops[1:]:
        largest = jnp.maximum(largest, top)
    factors = [jnp.exp2((top - largest) * SCALE) for top in tops]
    total = totals[0] * factors[0]
    num = rx_s[x].astype(F32) * factors[0] + suf_n * factors[1]
    for k in range(1, 5):
        total = total + totals[k] * factors[k]
    for k, xx in enumerate(x_peers):
        num = num + rx_r[xx].astype(F32) * factors[2 + k]
    for zz in range(NZ):
        rz_s[zz] = num[zz * 16 : (zz + 1) * 16].astype(BF16)
    rzml_s[0] = largest
    rzml_s[1] = total

    for zz in z_own:
        where = device(x, zz, c, y)
        for copy in (
            remote(rz_s.at[zz], rz_r.at[z], rz_ss.at[zz], rz_rs.at[z], where),
            remote(rzml_s, rzml_r.at[z], rzm_ss.at[zz], rzm_rs.at[z], where),
        ):
            copy.start()
            sends.append(copy)
    rz_r[z] = rz_s[z]
    rzml_r[z] = rzml_s[...]
    for zz in z_own:
        remote(rz_s.at[zz], rz_r.at[zz], rz_ss.at[zz], rz_rs.at[zz], sibling).wait_recv()
        remote(rzml_s, rzml_r.at[zz], rzm_ss.at[zz], rzm_rs.at[zz], sibling).wait_recv()
    tops = [rzml_r[zz, 0] for zz in range(NZ)]
    largest = tops[0]
    for top in tops[1:]:
        largest = jnp.maximum(largest, top)
    num, total = None, None
    for zz in range(NZ):
        factor = jnp.exp2((tops[zz] - largest) * SCALE)
        add_n, add_l = rz_r[zz].astype(F32) * factor, rzml_r[zz, 1] * factor
        num, total = (add_n, add_l) if zz == 0 else (num + add_n, total + add_l)
    az[z] = (num / total).astype(BF16)

    for zz in z_own:
        copy = remote(az.at[z], az.at[z], az_ss.at[zz], az_rs.at[z], device(x, zz, c, y))
        copy.start()
        sends.append(copy)
    for zz in z_own:
        remote(az.at[z], az.at[zz], az_ss.at[zz], az_rs.at[zz], sibling).wait_recv()
    ax[x] = dot_t(pick[...], az.reshape(HD, ROWS)[...]).astype(BF16)
    for xx in x_peers:
        copy = remote(ax.at[x], ax.at[x], ax_ss.at[xx], ax_rs.at[x], device(xx, z, c, y))
        copy.start()
        sends.append(copy)
    copy_wt.wait()
    swaps[3].wait_recv()

    def project(xx):
        attention = jnp.concatenate([ax[xx, pl.ds(j * 32, 32), :] for j in range(GROUP)], axis=1)
        for d in range(NC):
            ys[xx, d] = dot_t(attention, wt[d])

    def send_y(xx, d):
        cc = lax.rem(c + d, NC)
        return remote(
            ys.at[xx, d], yr.at[y, c], y_ss.at[xx, d], y_rs.at[y, c], device(x, z, cc, xx)
        )

    def finish(step, _):
        xx = lax.rem(x + lax.div(step * (step + 1), 2), NX)

        @pl.when(step > 0)
        def _():
            remote(ax.at[x], ax.at[xx], ax_ss.at[xx], ax_rs.at[xx], sibling).wait_recv()

        project(xx)

        @pl.when(xx == y)
        def _():
            yr[y, c] = ys[xx, 0]

        @pl.when(xx != y)
        def _():
            send_y(xx, 0).start()

        send_y(xx, 1).start()
        return 0

    lax.fori_loop(0, NX, finish, 0)
    for yy, cc in y_peers:
        remote(ys.at[0, 0], yr.at[yy, cc], y_ss.at[0, 0], y_rs.at[yy, cc], sibling).wait_recv()
    result = None
    for yy in range(NY):
        for cc in range(NC):
            result = yr[yy, cc] if result is None else result + yr[yy, cc]
    out_ref[...] = result

    for copy in sends:
        copy.wait_send()
    for xx in x_peers:
        remote(rx_s.at[xx], rx_r.at[x], rx_ss.at[xx], rx_rs.at[x], sibling).wait_send()
        remote(rxml_s.at[xx], rxml_r.at[x], rxm_ss.at[xx], rxm_rs.at[x], sibling).wait_send()
    for yy, cc in y_peers:
        d = lax.rem(c + cc, NC)
        remote(ys.at[yy, d], yr.at[y, c], y_ss.at[yy, d], y_rs.at[y, c], sibling).wait_send()


def local(queries, sys_cache, ctx_cache, block_context, context_id, suffix_cache, suffix_lengths, out_weight):
    split = queries.reshape(2, 16, HD).transpose(1, 0, 2)
    smem, anywhere = pl.BlockSpec(memory_space=pltpu.SMEM), pl.BlockSpec(memory_space=pl.ANY)
    dma = pltpu.SemaphoreType.DMA
    return pl.pallas_call(
        kernel,
        out_shape=jax.ShapeDtypeStruct((128 // NY, COLS), F32),
        in_specs=[smem] * 3 + [anywhere] * 5,
        out_specs=pl.BlockSpec(memory_space=pltpu.VMEM),
        scratch_shapes=[
            pltpu.VMEM((16, 2, HD), BF16),
            pltpu.VMEM((NX, SLOTS, GROUP, 2, HD), BF16),
            pltpu.VMEM((TOK, 2, HD), BF16),
            pltpu.VMEM((TOK, HD), BF16),
            pltpu.VMEM((VROWS, TOK), BF16),
            pltpu.VMEM((2, SUF_T, 2, 2 * HD), BF16),
            pltpu.VMEM((HD, 2 * HD), BF16),
            pltpu.VMEM((2 * SUF_T, HD), F32),
            pltpu.VMEM((2, HD, 2 * HD), F32),
            pltpu.VMEM((HD, HD), F32),
            pltpu.VMEM((2, 1, HD), F32),
            pltpu.VMEM((HD, HD), F32),
            pltpu.VMEM((2, 1, HD), F32),
            pltpu.VMEM((2, 1, HD), jnp.int32),
            pltpu.VMEM((2, 1, HD), jnp.int32),
            pltpu.VMEM((SLOTS, 1, HD), jnp.int32),
            pltpu.VMEM((NX, 2, 1, HD), jnp.int32),
            pltpu.VMEM((256, 256), BF16),
            pltpu.VMEM((256, 256), BF16),
            pltpu.VMEM((HD, HD), BF16),
            pltpu.VMEM((NX, HD, ROWS), BF16),
            pltpu.VMEM((NX, 2, 1, ROWS), F32),
            pltpu.VMEM((NX, HD, ROWS), BF16),
            pltpu.VMEM((NX, 2, 1, ROWS), F32),
            pltpu.VMEM((NZ, 16, ROWS), BF16),
            pltpu.VMEM((2, 1, ROWS), F32),
            pltpu.VMEM((NZ, 16, ROWS), BF16),
            pltpu.VMEM((NZ, 2, 1, ROWS), F32),
            pltpu.VMEM((NZ, 16, ROWS), BF16),
            pltpu.VMEM((NX, ROWS, HD), BF16),
            pltpu.VMEM((NC, COLS, GROUP * HD), BF16),
            pltpu.VMEM((NX, NC, 32, COLS), F32),
            pltpu.VMEM((NY, NC, 32, COLS), F32),
            dma((6,)), dma((6,)), dma((6,)),
            dma((SLOTS,)), dma((SLOTS,)), dma((SLOTS,)), dma((SLOTS,)),
            dma((NX,)), dma((NX,)), dma((NX,)), dma((NX,)),
            dma((NX,)), dma((NX,)), dma((NX,)), dma((NX,)),
            dma((NZ,)), dma((NZ,)), dma((NZ,)), dma((NZ,)),
            dma((NZ,)), dma((NZ,)), dma((NX,)), dma((NX,)),
            dma((NX, NC)), dma((NY, NC)),
        ],
        compiler_params=pltpu.CompilerParams(
            collective_id=0, has_side_effects=True, vmem_limit_bytes=48 * 1024 * 1024
        ),
        cost_estimate=pl.CostEstimate(flops=2 * 10**9, bytes_accessed=4 * 10**6, transcendentals=2 * 10**6),
    )(
        context_id, suffix_lengths, block_context, split, sys_cache, ctx_cache, suffix_cache, out_weight.T,
    )


def solution(mesh):
    return jax.shard_map(
        local,
        mesh=mesh,
        in_specs=(
            P("seq", "head"),
            P("seq", None, "head"),
            P("seq", None, "head"),
            P("seq"),
            P("seq"),
            P("seq", None, None, "head"),
            P("seq"),
            P("head", "seq"),
        ),
        out_specs=P("head", "seq"),
        check_vma=False,
    )
```

```python
import math

import jax
import jax.numpy as jnp
from jax import lax
from jax.experimental import pallas as pl
from jax.experimental.pallas import tpu as pltpu
from jax.sharding import PartitionSpec as P

HD = 128
NX, NZ, NC, NY = 4, 8, 2, 4
SLOTS = NZ * NC
GROUP = 8
ROWS = SLOTS * GROUP * 2
SYS_T, CTX_T, SUF_T = 64, 512, 1024
TOK = 2 * (SYS_T + CTX_T)
BLOCK = 256
COLS = 80
VROWS = HD + 16
SLICE = HD // NZ
LOG2E = math.log2(math.e)
SCALE = LOG2E / math.sqrt(HD)
LOW = -1e30
MASKED = -3e38
MESH = pl.DeviceIdType.MESH
F32, BF16 = jnp.float32, jnp.bfloat16
CHUNK = 512


def dot(a, b):
    return lax.dot_general(a, b, (((1,), (0,)), ((), ())), preferred_element_type=F32)


def dot_t(a, b):
    return lax.dot_general(a, b, (((1,), (1,)), ((), ())), preferred_element_type=F32)


def iota(shape, dim):
    return lax.broadcasted_iota(jnp.int32, shape, dim)


def kernel(
    cid_hbm, len_hbm, bc_hbm, q_hbm, sys_hbm, ctx_hbm, suf_hbm, wt_hbm, out_ref,
    cid_ref, len_ref, bc_ref, stage, qg, kvx, keys, vt, sufx, qbd, ssuf, nsuf, suf_s, sufml_s, suf_r, sufml_r, bc_s, bc_r,
    perm, eye, pick, tags, rs_s, lse_s, rs_r, lse_r, az, ax, wt, ys, yr,
    loc, small, sib_s, sib_r, zq_s, zq_r, xq_s, xq_r, rs_ss, rs_rs, lse_ss, lse_rs, az_ss, az_rs, ax_ss, ax_rs, y_ss, y_rs,
):
    seq, y = lax.axis_index("seq"), lax.axis_index("head")
    x, z, c = lax.div(seq, SLOTS), lax.rem(lax.div(seq, NC), NZ), lax.rem(seq, NC)
    o = 1 - c
    slot = z * NC + c

    def device(xx, zz, cc, yy):
        return ((xx * NZ + zz) * NC + cc, yy)

    def remote(src, dst, send, recv, where):
        return pltpu.make_async_remote_copy(
            src_ref=src, dst_ref=dst, send_sem=send, recv_sem=recv, device_id=where, device_id_type=MESH
        )

    def await_bytes(ref, sem):
        pltpu.make_async_copy(ref, ref, sem).wait()

    def loop(start, stop, body):
        def step(k, _):
            body(k)
            return 0

        lax.fori_loop(start, stop, step, 0)

    def far_first(k):
        half = lax.div(k + 1, 2)
        return lax.rem(4 + jnp.where(lax.rem(k, 2) == 1, half, -half), NZ)

    def near_first(k):
        half = lax.div(k + 1, 2)
        return lax.rem(NZ + jnp.where(lax.rem(k, 2) == 1, half, -half), NZ)

    def x_order(k):
        return lax.rem(lax.div(k * (k + 1), 2), NX)

    sibling = device(x, z, o, y)
    opposite = lax.rem(z + 4, NZ)

    barrier = pltpu.get_barrier_semaphore()

    def greet(where):
        pl.semaphore_signal(barrier, inc=1, device_id=where, device_id_type=MESH)

    def greet_z(k):
        zz = lax.rem(z + far_first(k), NZ)
        greet(device(x, zz, c, y))
        greet(device(x, zz, o, y))

    loop(0, NZ - 1, greet_z)
    greet(sibling)
    for d in (2, 1, 3):
        greet(device(lax.rem(x + d, NX), z, c, y))
        for cc in range(NC):
            greet(device(x, z, cc, lax.rem(y + d, NY)))
    partners = 2 * NZ - 1 + 3 + 6

    own_128 = pl.ds(pl.multiple_of(c * HD, HD), HD)
    other_128 = pl.ds(pl.multiple_of(o * HD, HD), HD)
    own_w = pl.ds(pl.multiple_of(c * GROUP * HD, HD), GROUP * HD)
    other_w = pl.ds(pl.multiple_of(o * GROUP * HD, HD), GROUP * HD)
    copy_len = pltpu.make_async_copy(len_hbm, len_ref, small.at[0])
    copy_cid = pltpu.make_async_copy(cid_hbm, cid_ref, small.at[1])
    copy_bc = pltpu.make_async_copy(bc_hbm, bc_ref, small.at[2])
    copy_q = [
        pltpu.make_async_copy(q_hbm.at[pl.ds(g * GROUP, GROUP)], stage.at[g, pl.ds(0, GROUP)], small.at[3 + g])
        for g in range(2)
    ]
    copy_suf = pltpu.make_async_copy(suf_hbm, sufx, loc.at[0])
    copy_ctx = pltpu.make_async_copy(ctx_hbm.at[:, :, own_128], kvx.at[pl.ds(2 * SYS_T, CTX_T)], loc.at[1])
    copy_sys = pltpu.make_async_copy(sys_hbm.at[:, :, own_128], kvx.at[pl.ds(0, SYS_T)], loc.at[2])
    copy_wt = pltpu.make_async_copy(wt_hbm.at[:, own_w], wt.at[pl.ds(0, COLS)], loc.at[3])
    for copy in (copy_len, copy_cid, copy_bc, *copy_q, copy_suf, copy_ctx, copy_sys, copy_wt):
        copy.start()

    row, col = iota((256, 256), 0), iota((256, 256), 1)
    perm[...] = (col == jnp.where(row < HD, 2 * row, 2 * (row - HD) + 1)).astype(F32).astype(BF16)
    rest = lax.rem(row, 32)
    pick[...] = (col == lax.div(rest, 2) * 16 + lax.div(row, 32) * 2 + lax.rem(rest, 2)).astype(F32).astype(BF16)
    tag, to = iota((SLOTS * 18, ROWS), 0), iota((SLOTS * 18, ROWS), 1)
    at_tag = (lax.div(tag, 18) == lax.div(to, 16)) & (lax.rem(tag, 18) == 16 + lax.rem(to, 2))
    tags[...] = at_tag.astype(F32).astype(BF16)
    eye[...] = (iota((HD, HD), 0) == iota((HD, HD), 1)).astype(F32).astype(BF16)
    vt[pl.ds(HD, 16), :] = jnp.ones((16, TOK), BF16)
    qbd[...] = jnp.zeros((HD // 2, 2, 2 * HD), BF16)
    nsuf[...] = jnp.zeros((2, HD, 2 * HD), F32)
    lane = iota((1, HD), 1)
    for copy in (copy_cid, copy_bc, copy_len, *copy_q):
        copy.wait()
    ids = jnp.where(iota((2, HD), 0) == 0, cid_ref[0], cid_ref[1]).astype(F32).astype(BF16)
    stage[0, GROUP] = ids
    stage[1, GROUP] = ids
    bc_s[0] = jnp.full((1, HD), bc_ref[0], jnp.int32)
    bc_s[1] = jnp.full((1, HD), bc_ref[1], jnp.int32)
    qbd[pl.ds(c * GROUP, GROUP), :, own_128] = stage[c, pl.ds(0, GROUP)]
    qbd[pl.ds(16 + c * GROUP, GROUP), :, other_128] = stage[o, pl.ds(0, GROUP)]
    first = lax.rem(lane, 2) == 0
    place = lax.div(lane, 16)
    valid = (place == c) | (place == 2 + c)
    live = jnp.where(valid, jnp.where(first, 2 * len_ref[0], 2 * len_ref[1]), 0)
    suf_rows = sufx.reshape(2, 2 * SUF_T, 2 * HD)
    spread = qbd.reshape(HD, 2 * HD)

    def suffix_scores(part, top):
        start = pl.multiple_of(part * CHUNK, CHUNK)
        one = dot_t(suf_rows[0, pl.ds(start, CHUNK), :], spread[...])
        two = dot_t(suf_rows[1, pl.ds(start, CHUNK), :], spread[...])
        at = iota((CHUNK, HD), 0)
        at = jnp.where(lax.rem(at, 2) == 0, at + start, 1 << 20)
        scores = jnp.where(at < live, jnp.where(first, one, two), MASKED)
        ssuf[pl.ds(start, CHUNK), :] = scores
        return jnp.maximum(top, jnp.max(scores, axis=0, keepdims=True))

    copy_suf.wait()
    m_suf = lax.fori_loop(0, 2 * SUF_T // CHUNK, suffix_scores, jnp.full((1, HD), LOW, F32))

    flat = kvx.reshape(2 * TOK, HD)

    def take_apart(part):
        pairs = flat[pl.ds(pl.multiple_of(part * 256, 256), 256), :]
        both = dot(perm[...], pairs).astype(BF16)
        start = pl.multiple_of(part * HD, HD)
        keys[pl.ds(start, HD), :] = both[:HD]
        vt[pl.ds(0, HD), pl.ds(start, HD)] = dot_t(eye[...], both[HD:]).astype(BF16)

    copy_ctx.wait()
    loop(1, 5, take_apart)

    pl.semaphore_wait(barrier, partners)
    copy_self = pltpu.make_async_copy(stage.at[c], qg.at[x, slot], zq_r.at[z])
    copy_self.start()

    def send_q(zz, cc):
        remote(stage.at[cc], qg.at[x, slot], zq_s, zq_r.at[z], device(x, zz, cc, y)).start()

    send_q(z, o)

    def send_z(k):
        zz = lax.rem(z + far_first(k), NZ)
        for cc in range(NC):
            send_q(zz, cc)

    loop(0, NZ - 1, send_z)

    swaps = [
        remote(sys_hbm.at[:, :, other_128], kvx.at[pl.ds(SYS_T, SYS_T)], sib_s.at[0], sib_r.at[0], sibling),
        remote(
            ctx_hbm.at[:, :, other_128], kvx.at[pl.ds(2 * SYS_T + CTX_T, CTX_T)], sib_s.at[1], sib_r.at[1], sibling
        ),
        remote(bc_s, bc_r, sib_s.at[2], sib_r.at[2], sibling),
        remote(wt_hbm.at[:, other_w], wt.at[pl.ds(COLS, COLS)], sib_s.at[5], sib_r.at[5], sibling),
    ]
    for copy in swaps:
        copy.start()

    def suffix_sums(part, total):
        start = pl.multiple_of(part * CHUNK, CHUNK)
        weights = jnp.exp2(ssuf[pl.ds(start, CHUNK), :] * SCALE - m_suf * SCALE)
        weights = weights.astype(BF16).astype(F32)
        turned = pltpu.roll(weights, 1, 0).T.astype(BF16)
        for i in range(2):
            nsuf[i] += dot(turned, suf_rows[i, pl.ds(start, CHUNK), :])
        return total + jnp.sum(weights, axis=0, keepdims=True)

    l_suf = lax.fori_loop(0, 2 * SUF_T // CHUNK, suffix_sums, jnp.zeros((1, HD), F32))
    l_suf = jnp.where(valid, l_suf, 1.0)
    lse_suf = jnp.where(valid, m_suf * SCALE + jnp.log(l_suf) * LOG2E, LOW)
    even = lax.rem(iota((HD, HD), 0), 2) == 0
    suf_s[...] = jnp.where(even, nsuf[0, :, other_128], nsuf[1, :, other_128]).T / l_suf
    sufml_s[...] = lse_suf
    o_suf = jnp.where(even, nsuf[0, :, own_128], nsuf[1, :, own_128]).T / l_suf
    swaps_suf = [
        remote(suf_s, suf_r, sib_s.at[3], sib_r.at[3], sibling),
        remote(sufml_s, sufml_r, sib_s.at[4], sib_r.at[4], sibling),
    ]
    for copy in swaps_suf:
        copy.start()

    def pass_q(k):
        zz = lax.rem(z + near_first(k), NZ)
        pairs = qg.at[x, pl.ds(zz * NC, NC)]
        await_bytes(pairs, zq_r.at[zz])
        for d in (2, 1, 3):
            remote(pairs, pairs, xq_s, xq_r.at[x], device(lax.rem(x + d, NX), z, c, y)).start()

    loop(0, 1, pass_q)
    copy_sys.wait()
    swaps[0].wait_recv()
    take_apart(0)
    loop(1, 3, pass_q)
    swaps[1].wait_recv()
    loop(5, 9, take_apart)
    loop(3, NZ, pass_q)
    for copy in (swaps[2], *swaps_suf):
        copy.wait_recv()

    def partial(xx):
        queries = jnp.concatenate(
            [qg.at[xx, k, pl.ds(0, GROUP)].reshape(16, HD)[...] for k in range(SLOTS)], axis=0
        )
        pickers = (iota((16, HD), 1) == 0).astype(F32).astype(BF16)
        ids = dot_t(pickers, qg.at[xx].reshape(SLOTS * 18, HD)[...]).astype(BF16)
        ids = dot(ids, tags[...])[:1]
        parts = []
        for b in range(5):
            start, size = (0, 2 * SYS_T) if b == 0 else (2 * SYS_T + (b - 1) * BLOCK, BLOCK)
            scores = dot_t(keys[pl.ds(start, size), :], queries)
            top = jnp.max(scores, axis=0, keepdims=True)
            weights = jnp.exp2(scores * SCALE - top * SCALE).astype(BF16)
            sums = dot(vt[:, pl.ds(start, size)], weights)
            if b > 0:
                if b <= 2:
                    ok = ids == bc_ref[b - 1].astype(F32)
                else:
                    theirs = bc_r[b - 3].astype(F32)
                    ok = ids == jnp.concatenate([theirs, theirs], axis=1)
                top = jnp.where(ok, top, LOW)
            parts.append((top, sums))
        largest = parts[0][0]
        for top, _ in parts[1:]:
            largest = jnp.maximum(largest, top)
        total = None
        for top, sums in parts:
            scaled = sums * jnp.exp2((top - largest) * SCALE)
            total = scaled if total is None else total + scaled
        weight = total[HD : HD + 1]
        return total[:HD] * (1.0 / weight), largest * SCALE + jnp.log(weight) * LOG2E

    def send_rs(xx, numerator, lse):
        for k in range(NZ):
            rs_s[xx, k] = numerator[k * SLICE : (k + 1) * SLICE].astype(BF16)
        lse_s[xx] = lse

        def to_z(k):
            zz = lax.rem(z + far_first(k), NZ)
            where = device(xx, zz, c, y)
            remote(rs_s.at[xx, zz], rs_r.at[x, z], rs_ss.at[xx], rs_rs, where).start()
            remote(lse_s.at[xx], lse_r.at[x, z], lse_ss.at[xx], lse_rs, where).start()

        loop(0, jnp.where(xx == x, NZ - 1, NZ), to_z)

    num, lse = partial(x)
    mine = place == c
    both_o = jnp.where(mine, o_suf, pltpu.roll(suf_r[...], HD - 32, 1))
    both_l = jnp.where(
        mine, jnp.broadcast_to(lse_suf, (8, HD)), pltpu.roll(jnp.broadcast_to(sufml_r[...], (8, HD)), HD - 32, 1)
    )
    shift = lax.rem(z, 4) * 32
    both_o, both_l = pltpu.roll(both_o, shift, 1), pltpu.roll(both_l, shift, 1)[:1]
    here = lax.div(iota((1, ROWS), 1), 32) == z
    o_two = jnp.concatenate([both_o, both_o], axis=1)
    l_two = jnp.where(here, jnp.concatenate([both_l, both_l], axis=1), LOW)
    largest = jnp.maximum(lse, l_two)
    w_one, w_two = jnp.exp2(lse - largest), jnp.exp2(l_two - largest)
    norm = 1.0 / (w_one + w_two)
    num = num * (w_one * norm) + jnp.where(here, o_two, 0.0) * (w_two * norm)
    send_rs(x, num, largest + jnp.log(w_one + w_two) * LOG2E)
    self_rs = [
        pltpu.make_async_copy(rs_s.at[x, z], rs_r.at[x, z], rs_rs),
        pltpu.make_async_copy(lse_s.at[x], lse_r.at[x, z], lse_rs),
    ]
    for copy in self_rs:
        copy.start()

    def other_x(k):
        xx = lax.rem(x + x_order(k), NX)
        await_bytes(qg.at[xx], xq_r.at[xx])
        send_rs(xx, *partial(xx))

    loop(1, NX, other_x)

    await_bytes(lse_r, lse_rs)
    lses = [lse_r[xx, zz] for xx in range(NX) for zz in range(NZ)]
    largest = lses[0]
    for one in lses[1:]:
        largest = jnp.maximum(largest, one)
    factors = [jnp.exp2(one - largest) for one in lses]
    total = factors[0]
    for one in factors[1:]:
        total = total + one
    norm = 1.0 / total
    await_bytes(rs_r, rs_rs)
    num = jnp.zeros((SLICE, ROWS), F32)
    for k in range(NX * NZ):
        num = num + rs_r[k // NZ, k % NZ].astype(F32) * factors[k]
    az[x, z] = (num * norm).astype(BF16)

    def send_a(zz, d, recv):
        where = device(lax.rem(x + d, NX), z if zz is None else zz, c, y)
        remote(az.at[x, z], az.at[x, z], az_ss, recv, where).start()

    for d in (2, 1, 3):
        send_a(opposite, d, ax_rs.at[x])
    loop(0, NZ - 1, lambda k: send_a(lax.rem(z + far_first(k), NZ), 0, az_rs.at[z]))
    for d in (2, 1, 3):
        send_a(None, d, ax_rs.at[x])

    def pass_a(k):
        zz = lax.rem(z + near_first(k), NZ)
        part = az.at[x, zz]
        await_bytes(part, az_rs.at[zz])
        for d in (2, 1, 3):
            remote(part, part, ax_ss, ax_rs.at[x], device(lax.rem(x + d, NX), z, c, y)).start()

    loop(1, NZ - 1, pass_a)
    await_bytes(az.at[x, opposite], az_rs.at[opposite])
    copy_wt.wait()
    swaps[3].wait_recv()

    def finish(k):
        xx = lax.rem(x + x_order(k), NX)

        @pl.when(k > 0)
        def _():
            await_bytes(az.at[xx], ax_rs.at[xx])

        ax[...] = dot_t(pick[...], az.at[xx].reshape(HD, ROWS)[...]).astype(BF16)
        attention = jnp.concatenate([ax[pl.ds(j * 32, 32), :] for j in range(GROUP)], axis=1)
        projected = dot_t(attention, wt[...])
        ys[xx, 0] = projected[:, :COLS]
        ys[xx, 1] = projected[:, COLS:]

        @pl.when(xx == y)
        def _():
            pltpu.make_async_copy(ys.at[xx, 0], yr.at[y, c], y_rs).start()

        @pl.when(xx != y)
        def _():
            remote(ys.at[xx, 0], yr.at[y, c], y_ss, y_rs, device(x, z, c, xx)).start()

        remote(ys.at[xx, 1], yr.at[y, c], y_ss, y_rs, device(x, z, o, xx)).start()

    loop(0, NX, finish)
    await_bytes(yr, y_rs)
    result = None
    for yy in range(NY):
        for cc in range(NC):
            result = yr[yy, cc] if result is None else result + yr[yy, cc]
    out_ref[...] = result

    for copy in (*swaps, *swaps_suf):
        copy.wait_send()
    await_bytes(qg.at[x, pl.ds(0, 15)], zq_s)
    await_bytes(qg.at[pl.ds(0, 3)], xq_s)
    for d in range(1, NX):
        xx = lax.rem(x + d, NX)
        await_bytes(rs_s.at[xx], rs_ss.at[xx])
        await_bytes(lse_r.at[xx], lse_ss.at[xx])
    await_bytes(rs_s.at[x, pl.ds(0, NZ - 1)], rs_ss.at[x])
    await_bytes(lse_r.at[x, pl.ds(0, NZ - 1)], lse_ss.at[x])
    await_bytes(az.at[x], az_ss)
    await_bytes(az.at[x, pl.ds(0, 5)], az_ss)
    for _ in range(3):
        await_bytes(az.at[x, pl.ds(0, 6)], ax_ss)
    await_bytes(ys.at[pl.ds(0, 3)], y_ss)
    await_bytes(ys.at[3, 0], y_ss)


def local(queries, sys_cache, ctx_cache, block_context, context_id, suffix_cache, suffix_lengths, out_weight):
    split = queries.reshape(2, 16, HD).transpose(1, 0, 2)
    anywhere = pl.BlockSpec(memory_space=pl.ANY)
    dma = pltpu.SemaphoreType.DMA
    return pl.pallas_call(
        kernel,
        out_shape=jax.ShapeDtypeStruct((128 // NY, COLS), F32),
        in_specs=[anywhere] * 8,
        out_specs=pl.BlockSpec(memory_space=pltpu.VMEM),
        scratch_shapes=[
            pltpu.SMEM((2,), jnp.int32),
            pltpu.SMEM((2,), jnp.int32),
            pltpu.SMEM((2,), jnp.int32),
            pltpu.VMEM((2, GROUP + 1, 2, HD), BF16),
            pltpu.VMEM((NX, SLOTS, GROUP + 1, 2, HD), BF16),
            pltpu.VMEM((TOK, 2, HD), BF16),
            pltpu.VMEM((TOK, HD), BF16),
            pltpu.VMEM((VROWS, TOK), BF16),
            pltpu.VMEM((2, SUF_T, 2, 2 * HD), BF16),
            pltpu.VMEM((HD // 2, 2, 2 * HD), BF16),
            pltpu.VMEM((2 * SUF_T, HD), F32),
            pltpu.VMEM((2, HD, 2 * HD), F32),
            pltpu.VMEM((HD, HD), F32),
            pltpu.VMEM((1, HD), F32),
            pltpu.VMEM((HD, HD), F32),
            pltpu.VMEM((1, HD), F32),
            pltpu.VMEM((2, 1, HD), jnp.int32),
            pltpu.VMEM((2, 1, HD), jnp.int32),
            pltpu.VMEM((256, 256), BF16),
            pltpu.VMEM((HD, HD), BF16),
            pltpu.VMEM((256, 256), BF16),
            pltpu.VMEM((SLOTS * 18, ROWS), BF16),
            pltpu.VMEM((NX, NZ, SLICE, ROWS), BF16),
            pltpu.VMEM((NX, 1, ROWS), F32),
            pltpu.VMEM((NX, NZ, SLICE, ROWS), BF16),
            pltpu.VMEM((NX, NZ, 1, ROWS), F32),
            pltpu.VMEM((NX, NZ, SLICE, ROWS), BF16),
            pltpu.VMEM((ROWS, HD), BF16),
            pltpu.VMEM((NC * COLS, GROUP * HD), BF16),
            pltpu.VMEM((NX, NC, 32, COLS), F32),
            pltpu.VMEM((NY, NC, 32, COLS), F32),
            dma((4,)),
            dma((5,)),
            dma((6,)), dma((6,)),
            dma, dma((NZ,)),
            dma, dma((NX,)),
            dma((NX,)), dma,
            dma((NX,)), dma,
            dma, dma((NZ,)),
            dma, dma((NX,)),
            dma, dma,
        ],
        compiler_params=pltpu.CompilerParams(
            collective_id=0, has_side_effects=True, vmem_limit_bytes=63 * 1024 * 1024
        ),
        cost_estimate=pl.CostEstimate(flops=2 * 10**9, bytes_accessed=4 * 10**6, transcendentals=2 * 10**6),
    )(
        context_id, suffix_lengths, block_context, split, sys_cache, ctx_cache, suffix_cache, out_weight.T,
    )


def solution(mesh):
    return jax.shard_map(
        local,
        mesh=mesh,
        in_specs=(
            P("seq", "head"),
            P("seq", None, "head"),
            P("seq", None, "head"),
            P("seq"),
            P("seq"),
            P("seq", None, None, "head"),
            P("seq"),
            P("head", "seq"),
        ),
        out_specs=P("head", "seq"),
        check_vma=False,
    )
```

```python
import math

import jax
import jax.numpy as jnp
from jax import lax
from jax.experimental import pallas as pl
from jax.experimental.pallas import tpu as pltpu
from jax.sharding import PartitionSpec as P

HD = 128
NX, NZ, NC, NY = 4, 8, 2, 4
SLOTS = NZ * NC
GROUP = 8
ROWS = SLOTS * GROUP * 2
SYS_T, CTX_T, SUF_T = 64, 512, 1024
TOK = 2 * (SYS_T + CTX_T)
BLOCK = 256
COLS = 80
VROWS = HD + 16
SLICE = HD // NZ
LOG2E = math.log2(math.e)
SCALE = LOG2E / math.sqrt(HD)
LOW = -1e30
MASKED = -3e38
MESH = pl.DeviceIdType.MESH
F32, BF16 = jnp.float32, jnp.bfloat16
CHUNK = 512


def dot(a, b):
    return lax.dot_general(a, b, (((1,), (0,)), ((), ())), preferred_element_type=F32)


def dot_t(a, b):
    return lax.dot_general(a, b, (((1,), (1,)), ((), ())), preferred_element_type=F32)


def iota(shape, dim):
    return lax.broadcasted_iota(jnp.int32, shape, dim)


def kernel(
    cid_hbm, len_hbm, bc_hbm, q_hbm, sys_hbm, ctx_hbm, suf_hbm, wt_hbm, out_ref,
    cid_ref, len_ref, bc_ref, stage, qg, kvx, keys, vt, sufx, qbd, ssuf, nsuf, own_num, suf_s, sufml_s, suf_r, sufml_r, bc_s, bc_r,
    perm, eye, pick, tags, rs_s, lse_s, rs_r, lse_r, az, ax, wt, ys,
    loc, small, sib_s, sib_r, zq_s, zq_r, xq_s, xq_r, rs_ss, rs_rs, lse_ss, lse_rs, az_ss, az_rs, ax_ss, ax_rs, y_ss, y_rs,
):
    seq, y = lax.axis_index("seq"), lax.axis_index("head")
    x, z, c = lax.div(seq, SLOTS), lax.rem(lax.div(seq, NC), NZ), lax.rem(seq, NC)
    o = 1 - c
    slot = z * NC + c

    def device(xx, zz, cc, yy):
        return ((xx * NZ + zz) * NC + cc, yy)

    def remote(src, dst, send, recv, where):
        return pltpu.make_async_remote_copy(
            src_ref=src, dst_ref=dst, send_sem=send, recv_sem=recv, device_id=where, device_id_type=MESH
        )

    def await_bytes(ref, sem):
        pltpu.make_async_copy(ref, ref, sem).wait()

    def loop(start, stop, body):
        def step(k, _):
            body(k)
            return 0

        lax.fori_loop(start, stop, step, 0)

    def far_first(k):
        half = lax.div(k + 1, 2)
        return lax.rem(4 + jnp.where(lax.rem(k, 2) == 1, half, -half), NZ)

    def near_first(k):
        half = lax.div(k + 1, 2)
        return lax.rem(NZ + jnp.where(lax.rem(k, 2) == 1, half, -half), NZ)

    sibling = device(x, z, o, y)
    opposite = lax.rem(z + 4, NZ)

    barrier = pltpu.get_barrier_semaphore()

    def greet(where):
        pl.semaphore_signal(barrier, inc=1, device_id=where, device_id_type=MESH)

    def greet_z(k):
        zz = lax.rem(z + far_first(k), NZ)
        greet(device(x, zz, c, y))
        greet(device(x, zz, o, y))

    loop(0, NZ - 1, greet_z)
    greet(sibling)
    for d in (2, 1, 3):
        greet(device(lax.rem(x + d, NX), z, c, y))
        for cc in range(NC):
            greet(device(x, z, cc, lax.rem(y + d, NY)))
    partners = 2 * NZ - 1 + 3 + 6

    own_128 = pl.ds(pl.multiple_of(c * HD, HD), HD)
    other_128 = pl.ds(pl.multiple_of(o * HD, HD), HD)
    own_w = pl.ds(pl.multiple_of(c * GROUP * HD, HD), GROUP * HD)
    other_w = pl.ds(pl.multiple_of(o * GROUP * HD, HD), GROUP * HD)
    copy_len = pltpu.make_async_copy(len_hbm, len_ref, small.at[0])
    copy_cid = pltpu.make_async_copy(cid_hbm, cid_ref, small.at[1])
    copy_bc = pltpu.make_async_copy(bc_hbm, bc_ref, small.at[2])
    copy_q = [
        pltpu.make_async_copy(q_hbm.at[pl.ds(g * GROUP, GROUP)], stage.at[g, pl.ds(0, GROUP)], small.at[3 + g])
        for g in range(2)
    ]
    copy_suf = pltpu.make_async_copy(suf_hbm, sufx, loc.at[0])
    copy_ctx = pltpu.make_async_copy(ctx_hbm.at[:, :, own_128], kvx.at[pl.ds(2 * SYS_T, CTX_T)], loc.at[1])
    copy_sys = pltpu.make_async_copy(sys_hbm.at[:, :, own_128], kvx.at[pl.ds(0, SYS_T)], loc.at[2])
    copy_wt = pltpu.make_async_copy(wt_hbm.at[:, own_w], wt.at[pl.ds(0, COLS)], loc.at[3])
    for copy in (copy_len, copy_cid, copy_bc, *copy_q, copy_suf, copy_ctx, copy_sys, copy_wt):
        copy.start()

    row, col = iota((256, 1), 0), iota((256, 256), 1)
    perm[...] = (col == jnp.where(row < HD, 2 * row, 2 * (row - HD) + 1)).astype(F32).astype(BF16)
    rest = row & 31
    pick[...] = (col == ((rest >> 1) << 4) + ((row >> 5) << 1) + (rest & 1)).astype(F32).astype(BF16)
    to = iota((1, ROWS), 1)
    tags[...] = (iota((SLOTS * 18, ROWS), 0) == (to >> 4) * 18 + 16 + (to & 1)).astype(F32).astype(BF16)
    eye[...] = (iota((HD, HD), 0) == iota((HD, HD), 1)).astype(F32).astype(BF16)
    vt[pl.ds(HD, 16), :] = jnp.ones((16, TOK), BF16)
    qbd[...] = jnp.zeros((HD // 2, 2, 2 * HD), BF16)
    nsuf[...] = jnp.zeros((2, HD, 2 * HD), F32)
    lane = iota((1, HD), 1)
    for copy in (copy_cid, copy_bc, copy_len, *copy_q):
        copy.wait()
    ids = jnp.where(iota((2, HD), 0) == 0, cid_ref[0], cid_ref[1]).astype(F32).astype(BF16)
    stage[0, GROUP] = ids
    stage[1, GROUP] = ids
    bc_s[0] = jnp.full((1, HD), bc_ref[0], jnp.int32)
    bc_s[1] = jnp.full((1, HD), bc_ref[1], jnp.int32)
    qbd[pl.ds(c * GROUP, GROUP), :, own_128] = stage[c, pl.ds(0, GROUP)]
    qbd[pl.ds(16 + c * GROUP, GROUP), :, other_128] = stage[o, pl.ds(0, GROUP)]
    first = lax.rem(lane, 2) == 0
    place = lax.div(lane, 16)
    valid = (place == c) | (place == 2 + c)
    live = jnp.where(valid, jnp.where(first, 2 * len_ref[0], 2 * len_ref[1]), 0)
    suf_rows = sufx.reshape(2, 2 * SUF_T, 2 * HD)
    spread = qbd.reshape(HD, 2 * HD)

    def suffix_scores(part, top):
        start = pl.multiple_of(part * CHUNK, CHUNK)
        one = dot_t(suf_rows[0, pl.ds(start, CHUNK), :], spread[...])
        two = dot_t(suf_rows[1, pl.ds(start, CHUNK), :], spread[...])
        at = iota((CHUNK, HD), 0)
        at = jnp.where(lax.rem(at, 2) == 0, at + start, 1 << 20)
        scores = jnp.where(at < live, jnp.where(first, one, two), MASKED)
        ssuf[pl.ds(start, CHUNK), :] = scores
        return jnp.maximum(top, jnp.max(scores, axis=0, keepdims=True))

    flat = kvx.reshape(2 * TOK, HD)

    def take_apart(part):
        pairs = flat[pl.ds(pl.multiple_of(part * 256, 256), 256), :]
        both = dot(perm[...], pairs).astype(BF16)
        start = pl.multiple_of(part * HD, HD)
        keys[pl.ds(start, HD), :] = both[:HD]
        vt[pl.ds(0, HD), pl.ds(start, HD)] = dot_t(eye[...], both[HD:]).astype(BF16)

    pl.semaphore_wait(barrier, partners)
    copy_self = pltpu.make_async_copy(stage.at[c], qg.at[x, slot], zq_r.at[z])
    copy_self.start()

    def send_q(zz, cc):
        remote(stage.at[cc], qg.at[x, slot], zq_s, zq_r.at[z], device(x, zz, cc, y)).start()

    send_q(z, o)

    def send_z(k):
        zz = lax.rem(z + far_first(k), NZ)
        for cc in range(NC):
            send_q(zz, cc)

    loop(0, NZ - 1, send_z)

    swaps = [
        remote(sys_hbm.at[:, :, other_128], kvx.at[pl.ds(SYS_T, SYS_T)], sib_s.at[0], sib_r.at[0], sibling),
        remote(
            ctx_hbm.at[:, :, other_128], kvx.at[pl.ds(2 * SYS_T + CTX_T, CTX_T)], sib_s.at[1], sib_r.at[1], sibling
        ),
        remote(bc_s, bc_r, sib_s.at[2], sib_r.at[2], sibling),
        remote(wt_hbm.at[:, other_w], wt.at[pl.ds(COLS, COLS)], sib_s.at[5], sib_r.at[5], sibling),
    ]
    for copy in swaps:
        copy.start()

    def pass_q(k):
        zz = lax.rem(z + near_first(k), NZ)
        pairs = qg.at[x, pl.ds(zz * NC, NC)]
        await_bytes(pairs, zq_r.at[zz])
        for d in (2, 1, 3):
            remote(pairs, pairs, xq_s, xq_r.at[x], device(lax.rem(x + d, NX), z, c, y)).start()

    copy_ctx.wait()
    loop(1, 5, take_apart)
    loop(0, 1, pass_q)
    copy_suf.wait()
    m_suf = lax.fori_loop(0, 2 * SUF_T // CHUNK, suffix_scores, jnp.full((1, HD), LOW, F32))
    loop(1, 3, pass_q)
    copy_sys.wait()
    swaps[0].wait_recv()
    swaps[1].wait_recv()
    take_apart(0)
    loop(5, 9, take_apart)
    loop(3, NZ, pass_q)
    swaps[2].wait_recv()

    def partial(xx):
        queries = jnp.concatenate(
            [qg.at[xx, k, pl.ds(0, GROUP)].reshape(16, HD)[...] for k in range(SLOTS)], axis=0
        )
        pickers = (iota((16, HD), 1) == 0).astype(F32).astype(BF16)
        ids = dot_t(pickers, qg.at[xx].reshape(SLOTS * 18, HD)[...]).astype(BF16)
        ids = dot(ids, tags[...])[:1]
        blocks, tops, owner = [], [], []
        for start in range(0, TOK, HD):
            blocks.append(dot_t(keys[pl.ds(start, HD), :], queries))
            tops.append(jnp.max(blocks[-1], axis=0, keepdims=True))
            owner.append(0 if start < 2 * SYS_T else 1 + (start - 2 * SYS_T) // BLOCK)
        ok = [ids == bc_ref[k].astype(F32) for k in range(2)]
        for k in range(2):
            theirs = bc_r[k].astype(F32)
            ok.append(ids == jnp.concatenate([theirs, theirs], axis=1))
        largest = tops[0]
        for top, b in zip(tops[1:], owner[1:]):
            largest = jnp.maximum(largest, jnp.where(ok[b - 1], top, LOW))
        scaled = largest * SCALE
        bounds = [scaled] + [jnp.where(one, scaled, -LOW) for one in ok]
        total = None
        for k, (scores, b) in enumerate(zip(blocks, owner)):
            weights = jnp.exp2(scores * SCALE - bounds[b]).astype(BF16)
            sums = dot(vt[:, pl.ds(k * HD, HD)], weights)
            total = sums if total is None else total + sums
        weight = total[HD : HD + 1]
        return total[:HD] * (1.0 / weight), scaled + jnp.log(weight) * LOG2E

    def send_rs(xx, numerator, lse):
        for k in range(NZ):
            rs_s[xx, k] = numerator[k * SLICE : (k + 1) * SLICE].astype(BF16)
        lse_s[xx] = lse

        def to_z(k):
            zz = lax.rem(z + far_first(k), NZ)
            where = device(xx, zz, c, y)
            remote(rs_s.at[xx, zz], rs_r.at[x, z], rs_ss.at[xx], rs_rs, where).start()
            remote(lse_s.at[xx], lse_r.at[x, z], lse_ss.at[xx], lse_rs, where).start()

        loop(0, jnp.where(xx == x, NZ - 1, NZ), to_z)

    own_num[...], lse_s[x] = partial(x)
    def suffix_sums(part, total):
        start = pl.multiple_of(part * CHUNK, CHUNK)
        weights = jnp.exp2(ssuf[pl.ds(start, CHUNK), :] * SCALE - m_suf * SCALE)
        weights = weights.astype(BF16).astype(F32)
        turned = pltpu.roll(weights, 1, 0).T.astype(BF16)
        for i in range(2):
            nsuf[i] += dot(turned, suf_rows[i, pl.ds(start, CHUNK), :])
        return total + jnp.sum(weights, axis=0, keepdims=True)

    l_suf = lax.fori_loop(0, 2 * SUF_T // CHUNK, suffix_sums, jnp.zeros((1, HD), F32))
    l_suf = jnp.where(valid, l_suf, 1.0)
    lse_suf = jnp.where(valid, m_suf * SCALE + jnp.log(l_suf) * LOG2E, LOW)
    even = lax.rem(iota((HD, HD), 0), 2) == 0
    suf_s[...] = jnp.where(even, nsuf[0, :, other_128], nsuf[1, :, other_128]).T / l_suf
    sufml_s[...] = lse_suf
    o_suf = jnp.where(even, nsuf[0, :, own_128], nsuf[1, :, own_128]).T / l_suf
    swaps_suf = [
        remote(suf_s, suf_r, sib_s.at[3], sib_r.at[3], sibling),
        remote(sufml_s, sufml_r, sib_s.at[4], sib_r.at[4], sibling),
    ]
    for copy in swaps_suf:
        copy.start()

    def other_x(k):
        xx = lax.rem(x + k, NX)
        await_bytes(qg.at[xx], xq_r.at[xx])
        send_rs(xx, *partial(xx))

    loop(1, NX, other_x)

    for copy in swaps_suf:
        copy.wait_recv()
    num, lse = own_num[...], lse_s[x]
    mine = place == c
    both_o = jnp.where(mine, o_suf, pltpu.roll(suf_r[...], HD - 32, 1))
    both_l = jnp.where(
        mine, jnp.broadcast_to(lse_suf, (8, HD)), pltpu.roll(jnp.broadcast_to(sufml_r[...], (8, HD)), HD - 32, 1)
    )
    shift = lax.rem(z, 4) * 32
    both_o, both_l = pltpu.roll(both_o, shift, 1), pltpu.roll(both_l, shift, 1)[:1]
    here = lax.div(iota((1, ROWS), 1), 32) == z
    o_two = jnp.concatenate([both_o, both_o], axis=1)
    l_two = jnp.where(here, jnp.concatenate([both_l, both_l], axis=1), LOW)
    largest = jnp.maximum(lse, l_two)
    w_one, w_two = jnp.exp2(lse - largest), jnp.exp2(l_two - largest)
    norm = 1.0 / (w_one + w_two)
    num = num * (w_one * norm) + jnp.where(here, o_two, 0.0) * (w_two * norm)
    send_rs(x, num, largest + jnp.log(w_one + w_two) * LOG2E)
    self_rs = [
        pltpu.make_async_copy(rs_s.at[x, z], rs_r.at[x, z], rs_rs),
        pltpu.make_async_copy(lse_s.at[x], lse_r.at[x, z], lse_rs),
    ]
    for copy in self_rs:
        copy.start()

    await_bytes(lse_r, lse_rs)
    lses = [lse_r[xx, zz] for xx in range(NX) for zz in range(NZ)]
    largest = lses[0]
    for one in lses[1:]:
        largest = jnp.maximum(largest, one)
    factors = [jnp.exp2(one - largest) for one in lses]
    total = factors[0]
    for one in factors[1:]:
        total = total + one
    norm = 1.0 / total
    await_bytes(rs_r, rs_rs)
    num = jnp.zeros((SLICE, ROWS), F32)
    for k in range(NX * NZ):
        num = num + rs_r[k // NZ, k % NZ].astype(F32) * factors[k]
    az[x, z] = (num * norm).astype(BF16)

    def send_a(zz, d, recv):
        where = device(lax.rem(x + d, NX), z if zz is None else zz, c, y)
        remote(az.at[x, z], az.at[x, z], az_ss, recv, where).start()

    for d in (2, 1, 3):
        send_a(opposite, d, ax_rs.at[x])
    loop(0, NZ - 1, lambda k: send_a(lax.rem(z + far_first(k), NZ), 0, az_rs.at[z]))
    for d in (2, 1, 3):
        send_a(None, d, ax_rs.at[x])

    def pass_a(k):
        zz = lax.rem(z + near_first(k), NZ)
        part = az.at[x, zz]
        await_bytes(part, az_rs.at[zz])
        for d in (2, 1, 3):
            remote(part, part, ax_ss, ax_rs.at[x], device(lax.rem(x + d, NX), z, c, y)).start()

    loop(1, NZ - 1, pass_a)
    await_bytes(az.at[x, opposite], az_rs.at[opposite])
    copy_wt.wait()
    swaps[3].wait_recv()

    def finish(xx):
        ax[...] = dot_t(pick[...], az.at[xx].reshape(HD, ROWS)[...]).astype(BF16)
        attention = jnp.concatenate([ax[pl.ds(j * 32, 32), :] for j in range(GROUP)], axis=1)
        projected = dot_t(attention, wt[...])
        ys[xx, 0] = projected[:, :COLS]
        ys[xx, 1] = projected[:, COLS:]

        @pl.when(xx == y)
        def _():
            pltpu.make_async_copy(ys.at[xx, 0], out_ref.at[y, c], y_rs).start()

        @pl.when(xx != y)
        def _():
            remote(ys.at[xx, 0], out_ref.at[y, c], y_ss, y_rs, device(x, z, c, xx)).start()

        remote(ys.at[xx, 1], out_ref.at[y, c], y_ss, y_rs, device(x, z, o, xx)).start()

    def finish_all(k):
        far = jnp.where(k == 1, 2, jnp.where(k == 2, 1, jnp.where(k == 3, 3, 0)))
        xx = jnp.where(k == 0, x, lax.rem(y + far, NY))

        @pl.when((k > 0) & (xx != x))
        def _():
            await_bytes(az.at[xx], ax_rs.at[xx])

        @pl.when((k == 0) | (xx != x))
        def _():
            finish(xx)

    loop(0, NX + 1, finish_all)
    await_bytes(out_ref, y_rs)

    for copy in (*swaps, *swaps_suf):
        copy.wait_send()
    await_bytes(qg.at[x, pl.ds(0, 15)], zq_s)
    await_bytes(qg.at[pl.ds(0, 3)], xq_s)
    for d in range(1, NX):
        xx = lax.rem(x + d, NX)
        await_bytes(rs_s.at[xx], rs_ss.at[xx])
        await_bytes(lse_r.at[xx], lse_ss.at[xx])
    await_bytes(rs_s.at[x, pl.ds(0, NZ - 1)], rs_ss.at[x])
    await_bytes(lse_r.at[x, pl.ds(0, NZ - 1)], lse_ss.at[x])
    await_bytes(az.at[x], az_ss)
    await_bytes(az.at[x, pl.ds(0, 5)], az_ss)
    for _ in range(3):
        await_bytes(az.at[x, pl.ds(0, 6)], ax_ss)
    await_bytes(ys.at[pl.ds(0, 3)], y_ss)
    await_bytes(ys.at[3, 0], y_ss)


def local(queries, sys_cache, ctx_cache, block_context, context_id, suffix_cache, suffix_lengths, out_weight):
    split = queries.reshape(2, 16, HD).transpose(1, 0, 2)
    anywhere = pl.BlockSpec(memory_space=pl.ANY)
    dma = pltpu.SemaphoreType.DMA
    parts = pl.pallas_call(
        kernel,
        out_shape=jax.ShapeDtypeStruct((NY, NC, 128 // NY, COLS), F32),
        in_specs=[anywhere] * 8,
        out_specs=anywhere,
        scratch_shapes=[
            pltpu.SMEM((2,), jnp.int32),
            pltpu.SMEM((2,), jnp.int32),
            pltpu.SMEM((2,), jnp.int32),
            pltpu.VMEM((2, GROUP + 1, 2, HD), BF16),
            pltpu.VMEM((NX, SLOTS, GROUP + 1, 2, HD), BF16),
            pltpu.VMEM((TOK, 2, HD), BF16),
            pltpu.VMEM((TOK, HD), BF16),
            pltpu.VMEM((VROWS, TOK), BF16),
            pltpu.VMEM((2, SUF_T, 2, 2 * HD), BF16),
            pltpu.VMEM((HD // 2, 2, 2 * HD), BF16),
            pltpu.VMEM((2 * SUF_T, HD), F32),
            pltpu.VMEM((2, HD, 2 * HD), F32),
            pltpu.VMEM((HD, ROWS), F32),
            pltpu.VMEM((HD, HD), F32),
            pltpu.VMEM((1, HD), F32),
            pltpu.VMEM((HD, HD), F32),
            pltpu.VMEM((1, HD), F32),
            pltpu.VMEM((2, 1, HD), jnp.int32),
            pltpu.VMEM((2, 1, HD), jnp.int32),
            pltpu.VMEM((256, 256), BF16),
            pltpu.VMEM((HD, HD), BF16),
            pltpu.VMEM((256, 256), BF16),
            pltpu.VMEM((SLOTS * 18, ROWS), BF16),
            pltpu.VMEM((NX, NZ, SLICE, ROWS), BF16),
            pltpu.VMEM((NX, 1, ROWS), F32),
            pltpu.VMEM((NX, NZ, SLICE, ROWS), BF16),
            pltpu.VMEM((NX, NZ, 1, ROWS), F32),
            pltpu.VMEM((NX, NZ, SLICE, ROWS), BF16),
            pltpu.VMEM((ROWS, HD), BF16),
            pltpu.VMEM((NC * COLS, GROUP * HD), BF16),
            pltpu.VMEM((NX, NC, 32, COLS), F32),
            dma((4,)),
            dma((5,)),
            dma((6,)), dma((6,)),
            dma, dma((NZ,)),
            dma, dma((NX,)),
            dma((NX,)), dma,
            dma((NX,)), dma,
            dma, dma((NZ,)),
            dma, dma((NX,)),
            dma, dma,
        ],
        compiler_params=pltpu.CompilerParams(
            collective_id=0, has_side_effects=True, vmem_limit_bytes=63 * 1024 * 1024
        ),
        cost_estimate=pl.CostEstimate(flops=2 * 10**9, bytes_accessed=4 * 10**6, transcendentals=2 * 10**6),
    )(
        context_id, suffix_lengths, block_context, split, sys_cache, ctx_cache, suffix_cache, out_weight.T,
    )
    return parts.sum((0, 1))


def solution(mesh):
    return jax.shard_map(
        local,
        mesh=mesh,
        in_specs=(
            P("seq", "head"),
            P("seq", None, "head"),
            P("seq", None, "head"),
            P("seq"),
            P("seq"),
            P("seq", None, None, "head"),
            P("seq"),
            P("head", "seq"),
        ),
        out_specs=P("head", "seq"),
        check_vma=False,
    )
```

```python
import math

import jax
import jax.numpy as jnp
from jax import lax
from jax.experimental import pallas as pl
from jax.experimental.pallas import tpu as pltpu
from jax.sharding import PartitionSpec as P

HD = 128
NX, NZ, NC, NY = 4, 8, 2, 4
SLOTS = NZ * NC
GROUP = 8
ROWS = SLOTS * GROUP * 2
SYS_T, CTX_T, SUF_T = 64, 512, 1024
TOK = 2 * (SYS_T + CTX_T)
BLOCK = 256
COLS, WIDE = 80, 128
VROWS = HD + 16
SLICE = HD // NZ
LOG2E = math.log2(math.e)
SCALE = LOG2E / math.sqrt(HD)
LOW = -1e30
MASKED = -3e38
MESH = pl.DeviceIdType.MESH
F32, BF16 = jnp.float32, jnp.bfloat16
CHUNK = 512


def dot(a, b):
    return lax.dot_general(a, b, (((1,), (0,)), ((), ())), preferred_element_type=F32)


def dot_t(a, b):
    return lax.dot_general(a, b, (((1,), (1,)), ((), ())), preferred_element_type=F32)


def iota(shape, dim):
    return lax.broadcasted_iota(jnp.int32, shape, dim)


FAR_FIRST = (4, 5, 3, 6, 2, 7, 1, 0)
NEAR_FIRST = (0, 1, 7, 2, 6, 3, 5, 4)


def kernel(
    cid_hbm, len_hbm, bc_hbm, q_hbm, sys_hbm, ctx_hbm, suf_hbm, wt_hbm, out_ref,
    cid_ref, len_ref, bc_ref, stage, qg, kvx, keys, vt, sufx, qbd, ssuf, nsuf, own_num, suf_s, sufml_s, suf_r, sufml_r, bc_s, bc_r,
    perm, eye, pick, tags, rs_s, lse_s, rs_r, lse_r, az, ax, wt, ys,
    loc, small, sib_s, sib_r, zq_s, zq_r, xq_s, xq_r, rs_ss, rs_rs, lse_ss, lse_rs, az_ss, ax_rs, y_ss, y_rs,
):
    seq, y = lax.axis_index("seq"), lax.axis_index("head")
    x, z, c = ((seq) >> 4), lax.rem(((seq) >> 1), NZ), ((seq) & 1)
    o = 1 - c
    slot = z * NC + c

    def device(xx, zz, cc, yy):
        return ((xx * NZ + zz) * NC + cc, yy)

    def remote(src, dst, send, recv, where):
        return pltpu.make_async_remote_copy(
            src_ref=src, dst_ref=dst, send_sem=send, recv_sem=recv, device_id=where, device_id_type=MESH
        )

    def await_bytes(ref, sem):
        pltpu.make_async_copy(ref, ref, sem).wait()

    def loop(start, stop, body):
        def step(k, _):
            body(k)
            return 0

        lax.fori_loop(start, stop, step, 0)

    sibling = device(x, z, o, y)

    barrier = pltpu.get_barrier_semaphore()

    def greet(where):
        pl.semaphore_signal(barrier, inc=1, device_id=where, device_id_type=MESH)

    def greet_z(k):
        zz = ((z + FAR_FIRST[k]) & 7)
        greet(device(x, zz, c, y))
        greet(device(x, zz, o, y))

    for k in range(NZ - 1):
        greet_z(k)
    greet(sibling)
    for d in (2, 1, 3):
        greet(device(((x + d) & 3), z, c, y))
        for cc in range(NC):
            greet(device(x, z, cc, ((y + d) & 3)))
    partners = 2 * NZ - 1 + 3 + 6

    own_128 = pl.ds(pl.multiple_of(c * HD, HD), HD)
    other_128 = pl.ds(pl.multiple_of(o * HD, HD), HD)
    own_w = pl.ds(pl.multiple_of(c * GROUP * HD, HD), GROUP * HD)
    other_w = pl.ds(pl.multiple_of(o * GROUP * HD, HD), GROUP * HD)
    copy_len = pltpu.make_async_copy(len_hbm, len_ref, small.at[0])
    copy_cid = pltpu.make_async_copy(cid_hbm, cid_ref, small.at[1])
    copy_bc = pltpu.make_async_copy(bc_hbm, bc_ref, small.at[2])
    copy_q = [
        pltpu.make_async_copy(q_hbm.at[pl.ds(g * GROUP, GROUP)], stage.at[g, pl.ds(0, GROUP)], small.at[3 + g])
        for g in range(2)
    ]
    copy_suf = pltpu.make_async_copy(suf_hbm, sufx, loc.at[0])
    copy_ctx = pltpu.make_async_copy(ctx_hbm.at[:, :, own_128], kvx.at[pl.ds(2 * SYS_T, CTX_T)], loc.at[1])
    copy_sys = pltpu.make_async_copy(sys_hbm.at[:, :, own_128], kvx.at[pl.ds(0, SYS_T)], loc.at[2])
    copy_wt = pltpu.make_async_copy(wt_hbm.at[:, own_w], wt.at[pl.ds(0, COLS)], loc.at[3])
    for copy in (copy_len, copy_cid, copy_bc, *copy_q, copy_suf, copy_ctx, copy_sys, copy_wt):
        copy.start()

    row, col = iota((256, 1), 0), iota((256, 256), 1)
    perm[...] = (col == jnp.where(row < HD, 2 * row, 2 * (row - HD) + 1)).astype(F32).astype(BF16)
    rest = row & 31
    pick[...] = (col == ((rest >> 1) << 4) + ((row >> 5) << 1) + (rest & 1)).astype(F32).astype(BF16)
    to = iota((1, ROWS), 1)
    tags[...] = (iota((SLOTS * 18, ROWS), 0) == (to >> 4) * 18 + 16 + (to & 1)).astype(F32).astype(BF16)
    eye[...] = (iota((HD, HD), 0) == iota((HD, HD), 1)).astype(F32).astype(BF16)
    vt[pl.ds(HD, 16), :] = jnp.ones((16, TOK), BF16)
    qbd[...] = jnp.zeros((HD // 2, 2, 2 * HD), BF16)
    nsuf[...] = jnp.zeros((2, HD, 2 * HD), F32)
    for k in range(NC):
        wt[pl.ds(k * WIDE + COLS, WIDE - COLS), :] = jnp.zeros((WIDE - COLS, GROUP * HD), BF16)
    lane = iota((1, HD), 1)
    for copy in (copy_cid, copy_bc, copy_len, *copy_q):
        copy.wait()
    ids = jnp.where(iota((2, HD), 0) == 0, cid_ref[0], cid_ref[1]).astype(F32).astype(BF16)
    stage[0, GROUP] = ids
    stage[1, GROUP] = ids
    bc_s[0] = jnp.full((1, HD), bc_ref[0], jnp.int32)
    bc_s[1] = jnp.full((1, HD), bc_ref[1], jnp.int32)
    qbd[pl.ds(c * GROUP, GROUP), :, own_128] = stage[c, pl.ds(0, GROUP)]
    qbd[pl.ds(16 + c * GROUP, GROUP), :, other_128] = stage[o, pl.ds(0, GROUP)]
    first = ((lane) & 1) == 0
    place = ((lane) >> 4)
    valid = (place == c) | (place == 2 + c)
    live = jnp.where(valid, jnp.where(first, 2 * len_ref[0], 2 * len_ref[1]), 0)
    suf_rows = sufx.reshape(2, 2 * SUF_T, 2 * HD)
    spread = qbd.reshape(HD, 2 * HD)

    def suffix_scores(part, top):
        start = pl.multiple_of(part * CHUNK, CHUNK)
        one = dot_t(suf_rows[0, pl.ds(start, CHUNK), :], spread[...])
        two = dot_t(suf_rows[1, pl.ds(start, CHUNK), :], spread[...])
        at = iota((CHUNK, HD), 0)
        at = jnp.where(((at) & 1) == 0, at + start, 1 << 20)
        scores = jnp.where(at < live, jnp.where(first, one, two), MASKED)
        ssuf[pl.ds(start, CHUNK), :] = scores
        return jnp.maximum(top, jnp.max(scores, axis=0, keepdims=True))

    flat = kvx.reshape(2 * TOK, HD)

    def take_apart(part):
        pairs = flat[pl.ds(pl.multiple_of(part * 256, 256), 256), :]
        both = dot(perm[...], pairs).astype(BF16)
        start = pl.multiple_of(part * HD, HD)
        keys[pl.ds(start, HD), :] = both[:HD]
        vt[pl.ds(0, HD), pl.ds(start, HD)] = dot_t(eye[...], both[HD:]).astype(BF16)

    pl.semaphore_wait(barrier, partners)
    copy_self = pltpu.make_async_copy(stage.at[c], qg.at[x, slot], zq_r.at[z])
    copy_self.start()

    def send_q(zz, cc):
        remote(stage.at[cc], qg.at[x, slot], zq_s, zq_r.at[z], device(x, zz, cc, y)).start()

    send_q(z, o)

    def send_z(k):
        zz = ((z + FAR_FIRST[k]) & 7)
        for cc in range(NC):
            send_q(zz, cc)

    for k in range(NZ - 1):
        send_z(k)

    swaps = [
        remote(sys_hbm.at[:, :, other_128], kvx.at[pl.ds(SYS_T, SYS_T)], sib_s.at[0], sib_r.at[0], sibling),
        remote(
            ctx_hbm.at[:, :, other_128], kvx.at[pl.ds(2 * SYS_T + CTX_T, CTX_T)], sib_s.at[1], sib_r.at[1], sibling
        ),
        remote(bc_s, bc_r, sib_s.at[2], sib_r.at[2], sibling),
        remote(wt_hbm.at[:, other_w], wt.at[pl.ds(WIDE, COLS)], sib_s.at[5], sib_r.at[5], sibling),
    ]
    for copy in swaps:
        copy.start()

    def pass_q(k):
        zz = ((z + NEAR_FIRST[k]) & 7)
        pairs = qg.at[x, pl.ds(zz * NC, NC)]
        await_bytes(pairs, zq_r.at[zz])
        for d in (2, 1, 3):
            remote(pairs, pairs, xq_s, xq_r.at[x], device(((x + d) & 3), z, c, y)).start()

    copy_ctx.wait()
    loop(1, 5, take_apart)
    copy_suf.wait()
    steps = 2 * SUF_T // CHUNK
    m_suf = jnp.full((1, HD), LOW, F32)
    for k in range(0, 1):
        pass_q(k)
    m_suf = lax.fori_loop(0, steps // 2, suffix_scores, m_suf)
    for k in range(1, 3):
        pass_q(k)
    m_suf = lax.fori_loop(steps // 2, 3 * steps // 4, suffix_scores, m_suf)
    for k in range(3, 5):
        pass_q(k)
    m_suf = lax.fori_loop(3 * steps // 4, steps, suffix_scores, m_suf)
    for k in range(5, 7):
        pass_q(k)
    copy_sys.wait()
    swaps[0].wait_recv()
    swaps[1].wait_recv()
    take_apart(0)
    loop(5, 9, take_apart)
    for k in range(7, 8):
        pass_q(k)
    swaps[2].wait_recv()

    def partial(xx):
        queries = jnp.concatenate(
            [qg.at[xx, k, pl.ds(0, GROUP)].reshape(16, HD)[...] for k in range(SLOTS)], axis=0
        )
        pickers = (iota((16, HD), 1) == 0).astype(F32).astype(BF16)
        ids = dot_t(pickers, qg.at[xx].reshape(SLOTS * 18, HD)[...]).astype(BF16)
        ids = dot(ids, tags[...])[:1]
        blocks, tops, owner = [], [], []
        for start in range(0, TOK, HD):
            blocks.append(dot_t(keys[pl.ds(start, HD), :], queries))
            tops.append(jnp.max(blocks[-1], axis=0, keepdims=True))
            owner.append(0 if start < 2 * SYS_T else 1 + (start - 2 * SYS_T) // BLOCK)
        ok = [ids == bc_ref[k].astype(F32) for k in range(2)]
        for k in range(2):
            theirs = bc_r[k].astype(F32)
            ok.append(ids == jnp.concatenate([theirs, theirs], axis=1))
        largest = tops[0]
        for top, b in zip(tops[1:], owner[1:]):
            largest = jnp.maximum(largest, jnp.where(ok[b - 1], top, LOW))
        scaled = largest * SCALE
        bounds = [scaled] + [jnp.where(one, scaled, -LOW) for one in ok]
        total = None
        for k, (scores, b) in enumerate(zip(blocks, owner)):
            weights = jnp.exp2(scores * SCALE - bounds[b]).astype(BF16)
            sums = dot(vt[:, pl.ds(k * HD, HD)], weights)
            total = sums if total is None else total + sums
        weight = total[HD : HD + 1]
        return total[:HD] * (1.0 / weight), scaled + jnp.log(weight) * LOG2E

    def send_rs(xx, numerator, lse, own=False):
        for k in range(NZ):
            rs_s[xx, k] = numerator[k * SLICE : (k + 1) * SLICE].astype(BF16)
        lse_s[xx] = lse

        def to_z(k):
            zz = ((z + FAR_FIRST[k]) & 7)
            where = device(xx, zz, c, y)
            remote(rs_s.at[xx, zz], rs_r.at[x, z], rs_ss.at[xx], rs_rs, where).start()
            remote(lse_s.at[xx], lse_r.at[x, z], lse_ss.at[xx], lse_rs, where).start()

        for k in range(NZ - 1 if own else NZ):
            to_z(k)

    own_num[...], lse_s[x] = partial(x)
    def suffix_sums(part, total):
        start = pl.multiple_of(part * CHUNK, CHUNK)
        weights = jnp.exp2(ssuf[pl.ds(start, CHUNK), :] * SCALE - m_suf * SCALE)
        weights = weights.astype(BF16).astype(F32)
        turned = pltpu.roll(weights, 1, 0).T.astype(BF16)
        for i in range(2):
            nsuf[i] += dot(turned, suf_rows[i, pl.ds(start, CHUNK), :])
        return total + jnp.sum(weights, axis=0, keepdims=True)

    l_suf = lax.fori_loop(0, 2 * SUF_T // CHUNK, suffix_sums, jnp.zeros((1, HD), F32))
    l_suf = jnp.where(valid, l_suf, 1.0)
    lse_suf = jnp.where(valid, m_suf * SCALE + jnp.log(l_suf) * LOG2E, LOW)
    even = lax.rem(iota((HD, HD), 0), 2) == 0
    suf_s[...] = jnp.where(even, nsuf[0, :, other_128], nsuf[1, :, other_128]).T / l_suf
    sufml_s[...] = lse_suf
    o_suf = jnp.where(even, nsuf[0, :, own_128], nsuf[1, :, own_128]).T / l_suf
    swaps_suf = [
        remote(suf_s, suf_r, sib_s.at[3], sib_r.at[3], sibling),
        remote(sufml_s, sufml_r, sib_s.at[4], sib_r.at[4], sibling),
    ]
    for copy in swaps_suf:
        copy.start()

    def other_x(k):
        xx = ((x + k) & 3)
        await_bytes(qg.at[xx], xq_r.at[xx])
        send_rs(xx, *partial(xx))

    loop(1, NX, other_x)

    for copy in swaps_suf:
        copy.wait_recv()
    num, lse = own_num[...], lse_s[x]
    mine = place == c
    both_o = jnp.where(mine, o_suf, pltpu.roll(suf_r[...], HD - 32, 1))
    both_l = jnp.where(
        mine, jnp.broadcast_to(lse_suf, (8, HD)), pltpu.roll(jnp.broadcast_to(sufml_r[...], (8, HD)), HD - 32, 1)
    )
    shift = ((z) & 3) * 32
    both_o, both_l = pltpu.roll(both_o, shift, 1), pltpu.roll(both_l, shift, 1)[:1]
    here = lax.div(iota((1, ROWS), 1), 32) == z
    o_two = jnp.concatenate([both_o, both_o], axis=1)
    l_two = jnp.where(here, jnp.concatenate([both_l, both_l], axis=1), LOW)
    largest = jnp.maximum(lse, l_two)
    w_one, w_two = jnp.exp2(lse - largest), jnp.exp2(l_two - largest)
    norm = 1.0 / (w_one + w_two)
    num = num * (w_one * norm) + jnp.where(here, o_two, 0.0) * (w_two * norm)
    send_rs(x, num, largest + jnp.log(w_one + w_two) * LOG2E, own=True)
    self_rs = [
        pltpu.make_async_copy(rs_s.at[x, z], rs_r.at[x, z], rs_rs),
        pltpu.make_async_copy(lse_s.at[x], lse_r.at[x, z], lse_rs),
    ]
    for copy in self_rs:
        copy.start()

    await_bytes(lse_r, lse_rs)
    lses = [lse_r[xx, zz] for xx in range(NX) for zz in range(NZ)]
    largest = lses[0]
    for one in lses[1:]:
        largest = jnp.maximum(largest, one)
    factors = [jnp.exp2(one - largest) for one in lses]
    total = factors[0]
    for one in factors[1:]:
        total = total + one
    norm = 1.0 / total
    await_bytes(rs_r, rs_rs)
    num = jnp.zeros((SLICE, ROWS), F32)
    for k in range(NX * NZ):
        num = num + rs_r[k // NZ, k % NZ].astype(F32) * factors[k]
    az[x, z] = (num * norm).astype(BF16)

    def send_a(k):
        zz = ((z + FAR_FIRST[k]) & 7)
        for d in (2, 1, 3):
            remote(az.at[x, z], az.at[x, z], az_ss, ax_rs.at[x], device(((x + d) & 3), zz, c, y)).start()

        if k < NZ - 1:
            remote(az.at[x, z], az.at[x, z], az_ss, ax_rs.at[x], device(x, zz, c, y)).start()

    for k in range(NZ):
        send_a(k)
    await_bytes(az.at[x, pl.ds(0, NZ - 1)], ax_rs.at[x])
    copy_wt.wait()
    swaps[3].wait_recv()

    def finish(xx):
        ax[...] = dot_t(pick[...], az.at[xx].reshape(HD, ROWS)[...]).astype(BF16)
        attention = jnp.concatenate([ax[pl.ds(j * 32, 32), :] for j in range(GROUP)], axis=1)
        projected = dot_t(attention, wt[...])
        ys[xx, 0] = projected[:, :WIDE]
        ys[xx, 1] = projected[:, WIDE:]

        @pl.when(xx == y)
        def _():
            pltpu.make_async_copy(ys.at[xx, 0], out_ref.at[y, c], y_rs).start()

        @pl.when(xx != y)
        def _():
            remote(ys.at[xx, 0], out_ref.at[y, c], y_ss, y_rs, device(x, z, c, xx)).start()

        remote(ys.at[xx, 1], out_ref.at[y, c], y_ss, y_rs, device(x, z, o, xx)).start()

    def finish_all(k):
        far = jnp.where(k == 1, 2, jnp.where(k == 2, 1, jnp.where(k == 3, 3, 0)))
        xx = jnp.where(k == 0, x, ((y + far) & 3))

        @pl.when((k > 0) & (xx != x))
        def _():
            await_bytes(az.at[xx], ax_rs.at[xx])

        @pl.when((k == 0) | (xx != x))
        def _():
            finish(xx)

    loop(0, NX + 1, finish_all)
    await_bytes(out_ref, y_rs)

    for copy in (*swaps, *swaps_suf):
        copy.wait_send()
    await_bytes(qg.at[x, pl.ds(0, 15)], zq_s)
    await_bytes(qg.at[pl.ds(0, 3)], xq_s)
    for d in range(1, NX):
        xx = ((x + d) & 3)
        await_bytes(rs_s.at[xx], rs_ss.at[xx])
        await_bytes(lse_r.at[xx], lse_ss.at[xx])
    await_bytes(rs_s.at[x, pl.ds(0, NZ - 1)], rs_ss.at[x])
    await_bytes(lse_r.at[x, pl.ds(0, NZ - 1)], lse_ss.at[x])
    await_bytes(az.at[pl.ds(0, 3)], az_ss)
    await_bytes(az.at[x, pl.ds(0, NZ - 1)], az_ss)
    await_bytes(ys.at[pl.ds(0, 3)], y_ss)
    await_bytes(ys.at[3, 0], y_ss)


def local(queries, sys_cache, ctx_cache, block_context, context_id, suffix_cache, suffix_lengths, out_weight):
    split = queries.reshape(2, 16, HD).transpose(1, 0, 2)
    anywhere = pl.BlockSpec(memory_space=pl.ANY)
    dma = pltpu.SemaphoreType.DMA
    parts = pl.pallas_call(
        kernel,
        out_shape=jax.ShapeDtypeStruct((NY, NC, 128 // NY, WIDE), F32),
        in_specs=[anywhere] * 8,
        out_specs=anywhere,
        scratch_shapes=[
            pltpu.SMEM((2,), jnp.int32),
            pltpu.SMEM((2,), jnp.int32),
            pltpu.SMEM((2,), jnp.int32),
            pltpu.VMEM((2, GROUP + 1, 2, HD), BF16),
            pltpu.VMEM((NX, SLOTS, GROUP + 1, 2, HD), BF16),
            pltpu.VMEM((TOK, 2, HD), BF16),
            pltpu.VMEM((TOK, HD), BF16),
            pltpu.VMEM((VROWS, TOK), BF16),
            pltpu.VMEM((2, SUF_T, 2, 2 * HD), BF16),
            pltpu.VMEM((HD // 2, 2, 2 * HD), BF16),
            pltpu.VMEM((2 * SUF_T, HD), F32),
            pltpu.VMEM((2, HD, 2 * HD), F32),
            pltpu.VMEM((HD, ROWS), F32),
            pltpu.VMEM((HD, HD), F32),
            pltpu.VMEM((1, HD), F32),
            pltpu.VMEM((HD, HD), F32),
            pltpu.VMEM((1, HD), F32),
            pltpu.VMEM((2, 1, HD), jnp.int32),
            pltpu.VMEM((2, 1, HD), jnp.int32),
            pltpu.VMEM((256, 256), BF16),
            pltpu.VMEM((HD, HD), BF16),
            pltpu.VMEM((256, 256), BF16),
            pltpu.VMEM((SLOTS * 18, ROWS), BF16),
            pltpu.VMEM((NX, NZ, SLICE, ROWS), BF16),
            pltpu.VMEM((NX, 1, ROWS), F32),
            pltpu.VMEM((NX, NZ, SLICE, ROWS), BF16),
            pltpu.VMEM((NX, NZ, 1, ROWS), F32),
            pltpu.VMEM((NX, NZ, SLICE, ROWS), BF16),
            pltpu.VMEM((ROWS, HD), BF16),
            pltpu.VMEM((NC * WIDE, GROUP * HD), BF16),
            pltpu.VMEM((NX, NC, 32, WIDE), F32),
            dma((4,)),
            dma((5,)),
            dma((6,)), dma((6,)),
            dma, dma((NZ,)),
            dma, dma((NX,)),
            dma((NX,)), dma,
            dma((NX,)), dma,
            dma, dma((NX,)),
            dma, dma,
        ],
        compiler_params=pltpu.CompilerParams(
            collective_id=0, has_side_effects=True, vmem_limit_bytes=63 * 1024 * 1024
        ),
        cost_estimate=pl.CostEstimate(flops=2 * 10**9, bytes_accessed=4 * 10**6, transcendentals=2 * 10**6),
    )(
        context_id, suffix_lengths, block_context, split, sys_cache, ctx_cache, suffix_cache, out_weight.T,
    )
    return parts[..., :COLS].sum((0, 1))


def solution(mesh):
    return jax.shard_map(
        local,
        mesh=mesh,
        in_specs=(
            P("seq", "head"),
            P("seq", None, "head"),
            P("seq", None, "head"),
            P("seq"),
            P("seq"),
            P("seq", None, None, "head"),
            P("seq"),
            P("head", "seq"),
        ),
        out_specs=P("head", "seq"),
        check_vma=False,
    )
```

```python
import math

import jax
import jax.numpy as jnp
from jax import lax
from jax.experimental import pallas as pl
from jax.experimental.pallas import tpu as pltpu
from jax.sharding import PartitionSpec as P

HD = 128
NX, NZ, NC, NY = 4, 8, 2, 4
SLOTS = NZ * NC
GROUP = 8
ROWS = SLOTS * GROUP * 2
SYS_T, CTX_T, SUF_T = 64, 512, 1024
TOK = 2 * (SYS_T + CTX_T)
BLOCK = 256
COLS, WIDE = 80, 128
VROWS = HD + 16
SLICE = HD // NZ
LOG2E = math.log2(math.e)
SCALE = LOG2E / math.sqrt(HD)
LOW = -1e30
MASKED = -3e38
MESH = pl.DeviceIdType.MESH
F32, BF16 = jnp.float32, jnp.bfloat16
CHUNK = 512


def dot(a, b):
    return lax.dot_general(a, b, (((1,), (0,)), ((), ())), preferred_element_type=F32)


def dot_t(a, b):
    return lax.dot_general(a, b, (((1,), (1,)), ((), ())), preferred_element_type=F32)


def iota(shape, dim):
    return lax.broadcasted_iota(jnp.int32, shape, dim)


FAR_FIRST = (4, 5, 3, 6, 2, 7, 1, 0)
NEAR_FIRST = (0, 1, 7, 2, 6, 3, 5, 4)


def kernel(
    cid_hbm, len_hbm, bc_hbm, q_hbm, sys_hbm, ctx_hbm, suf_hbm, wt_hbm, out_ref,
    cid_ref, len_ref, bc_ref, stage, qg, kvx, keys, vt, sufx, qbd, ssuf, nsuf, own_num, suf_s, sufml_s, suf_r, sufml_r, bc_s, bc_r,
    perm, eye, pick, tags, rs_s, lse_s, rs_r, lse_r, az, ax, wt, ys,
    loc, small, sib_s, sib_r, zq_s, zq_r, xq_s, xq_r, rs_ss, rs_rs, lse_ss, lse_rs, az_ss, ax_rs, y_ss, y_rs,
):
    seq, y = lax.axis_index("seq"), lax.axis_index("head")
    x, z, c = ((seq) >> 4), lax.rem(((seq) >> 1), NZ), ((seq) & 1)
    o = 1 - c
    slot = z * NC + c

    def device(xx, zz, cc, yy):
        return ((xx * NZ + zz) * NC + cc, yy)

    def remote(src, dst, send, recv, where):
        return pltpu.make_async_remote_copy(
            src_ref=src, dst_ref=dst, send_sem=send, recv_sem=recv, device_id=where, device_id_type=MESH
        )

    def await_bytes(ref, sem):
        pltpu.make_async_copy(ref, ref, sem).wait()

    def loop(start, stop, body):
        def step(k, _):
            body(k)
            return 0

        lax.fori_loop(start, stop, step, 0)

    sibling = device(x, z, o, y)

    barrier = pltpu.get_barrier_semaphore()

    def greet(where):
        pl.semaphore_signal(barrier, inc=1, device_id=where, device_id_type=MESH)

    def greet_z(k):
        zz = ((z + FAR_FIRST[k]) & 7)
        greet(device(x, zz, c, y))
        greet(device(x, zz, o, y))

    for k in range(NZ - 1):
        greet_z(k)
    greet(sibling)
    for d in (2, 1, 3):
        greet(device(((x + d) & 3), z, c, y))
        for cc in range(NC):
            greet(device(x, z, cc, ((y + d) & 3)))
    partners = 2 * NZ - 1 + 3 + 6

    own_128 = pl.ds(pl.multiple_of(c * HD, HD), HD)
    other_128 = pl.ds(pl.multiple_of(o * HD, HD), HD)
    own_w = pl.ds(pl.multiple_of(c * GROUP * HD, HD), GROUP * HD)
    other_w = pl.ds(pl.multiple_of(o * GROUP * HD, HD), GROUP * HD)
    copy_len = pltpu.make_async_copy(len_hbm, len_ref, small.at[0])
    copy_cid = pltpu.make_async_copy(cid_hbm, cid_ref, small.at[1])
    copy_bc = pltpu.make_async_copy(bc_hbm, bc_ref, small.at[2])
    copy_q = [
        pltpu.make_async_copy(q_hbm.at[pl.ds(g * GROUP, GROUP)], stage.at[g, pl.ds(0, GROUP)], small.at[3 + g])
        for g in range(2)
    ]
    copy_suf = pltpu.make_async_copy(suf_hbm, sufx, loc.at[0])
    copy_ctx = pltpu.make_async_copy(ctx_hbm.at[:, :, own_128], kvx.at[pl.ds(2 * SYS_T, CTX_T)], loc.at[1])
    copy_sys = pltpu.make_async_copy(sys_hbm.at[:, :, own_128], kvx.at[pl.ds(0, SYS_T)], loc.at[2])
    copy_wt = pltpu.make_async_copy(wt_hbm.at[:, own_w], wt.at[pl.ds(0, COLS)], loc.at[3])
    for copy in (copy_len, copy_cid, copy_bc, *copy_q, copy_suf, copy_ctx, copy_sys, copy_wt):
        copy.start()

    qbd[...] = jnp.zeros((HD // 2, 2, 2 * HD), BF16)
    lane = iota((1, HD), 1)
    for copy in (copy_cid, copy_bc, copy_len, *copy_q):
        copy.wait()
    ids = jnp.where(iota((2, HD), 0) == 0, cid_ref[0], cid_ref[1]).astype(F32).astype(BF16)
    stage[0, GROUP] = ids
    stage[1, GROUP] = ids
    bc_s[0] = jnp.full((1, HD), bc_ref[0], jnp.int32)
    bc_s[1] = jnp.full((1, HD), bc_ref[1], jnp.int32)
    qbd[pl.ds(c * GROUP, GROUP), :, own_128] = stage[c, pl.ds(0, GROUP)]
    qbd[pl.ds(16 + c * GROUP, GROUP), :, other_128] = stage[o, pl.ds(0, GROUP)]
    first = ((lane) & 1) == 0
    place = ((lane) >> 4)
    valid = (place == c) | (place == 2 + c)
    live = jnp.where(valid, jnp.where(first, 2 * len_ref[0], 2 * len_ref[1]), 0)
    suf_rows = sufx.reshape(2, 2 * SUF_T, 2 * HD)
    spread = qbd.reshape(HD, 2 * HD)

    def suffix_scores(part, top):
        start = pl.multiple_of(part * CHUNK, CHUNK)
        one = dot_t(suf_rows[0, pl.ds(start, CHUNK), :], spread[...])
        two = dot_t(suf_rows[1, pl.ds(start, CHUNK), :], spread[...])
        at = iota((CHUNK, HD), 0)
        at = jnp.where(((at) & 1) == 0, at + start, 1 << 20)
        scores = jnp.where(at < live, jnp.where(first, one, two), MASKED)
        ssuf[pl.ds(start, CHUNK), :] = scores
        return jnp.maximum(top, jnp.max(scores, axis=0, keepdims=True))

    flat = kvx.reshape(2 * TOK, HD)

    def take_apart(part):
        pairs = flat[pl.ds(pl.multiple_of(part * 256, 256), 256), :]
        both = dot(perm[...], pairs).astype(BF16)
        start = pl.multiple_of(part * HD, HD)
        keys[pl.ds(start, HD), :] = both[:HD]
        vt[pl.ds(0, HD), pl.ds(start, HD)] = dot_t(eye[...], both[HD:]).astype(BF16)

    pl.semaphore_wait(barrier, partners)
    copy_self = pltpu.make_async_copy(stage.at[c], qg.at[x, slot], zq_r.at[z])
    copy_self.start()

    def send_q(zz, cc):
        remote(stage.at[cc], qg.at[x, slot], zq_s, zq_r.at[z], device(x, zz, cc, y)).start()

    send_q(z, o)

    def send_z(k):
        zz = ((z + FAR_FIRST[k]) & 7)
        for cc in range(NC):
            send_q(zz, cc)

    for k in range(NZ - 1):
        send_z(k)

    swaps = [
        remote(sys_hbm.at[:, :, other_128], kvx.at[pl.ds(SYS_T, SYS_T)], sib_s.at[0], sib_r.at[0], sibling),
        remote(
            ctx_hbm.at[:, :, other_128], kvx.at[pl.ds(2 * SYS_T + CTX_T, CTX_T)], sib_s.at[1], sib_r.at[1], sibling
        ),
        remote(bc_s, bc_r, sib_s.at[2], sib_r.at[2], sibling),
        remote(wt_hbm.at[:, other_w], wt.at[pl.ds(WIDE, COLS)], sib_s.at[5], sib_r.at[5], sibling),
    ]
    for copy in swaps:
        copy.start()

    row, col = iota((256, 1), 0), iota((256, 256), 1)
    perm[...] = (col == jnp.where(row < HD, 2 * row, 2 * (row - HD) + 1)).astype(F32).astype(BF16)
    rest = row & 31
    pick[...] = (col == ((rest >> 1) << 4) + ((row >> 5) << 1) + (rest & 1)).astype(F32).astype(BF16)
    to = iota((1, ROWS), 1)
    tags[...] = (iota((SLOTS * 18, ROWS), 0) == (to >> 4) * 18 + 16 + (to & 1)).astype(F32).astype(BF16)
    eye[...] = (iota((HD, HD), 0) == iota((HD, HD), 1)).astype(F32).astype(BF16)
    vt[pl.ds(HD, 16), :] = jnp.ones((16, TOK), BF16)
    nsuf[...] = jnp.zeros((2, HD, 2 * HD), F32)
    for k in range(NC):
        wt[pl.ds(k * WIDE + COLS, WIDE - COLS), :] = jnp.zeros((WIDE - COLS, GROUP * HD), BF16)

    def pass_q(k):
        zz = ((z + NEAR_FIRST[k]) & 7)
        pairs = qg.at[x, pl.ds(zz * NC, NC)]
        await_bytes(pairs, zq_r.at[zz])
        for d in (2, 1, 3):
            remote(pairs, pairs, xq_s, xq_r.at[x], device(((x + d) & 3), z, c, y)).start()

    copy_ctx.wait()
    loop(1, 5, take_apart)
    copy_suf.wait()
    steps = 2 * SUF_T // CHUNK
    m_suf = jnp.full((1, HD), LOW, F32)
    for k in range(0, 1):
        pass_q(k)
    m_suf = lax.fori_loop(0, steps // 2, suffix_scores, m_suf)
    for k in range(1, 3):
        pass_q(k)
    m_suf = lax.fori_loop(steps // 2, 3 * steps // 4, suffix_scores, m_suf)
    for k in range(3, 5):
        pass_q(k)
    m_suf = lax.fori_loop(3 * steps // 4, steps, suffix_scores, m_suf)
    for k in range(5, 7):
        pass_q(k)
    copy_sys.wait()
    swaps[0].wait_recv()
    swaps[1].wait_recv()
    take_apart(0)
    loop(5, 9, take_apart)
    for k in range(7, 8):
        pass_q(k)
    swaps[2].wait_recv()

    def partial(xx):
        queries = jnp.concatenate(
            [qg.at[xx, k, pl.ds(0, GROUP)].reshape(16, HD)[...] for k in range(SLOTS)], axis=0
        )
        pickers = (iota((16, HD), 1) == 0).astype(F32).astype(BF16)
        ids = dot_t(pickers, qg.at[xx].reshape(SLOTS * 18, HD)[...]).astype(BF16)
        ids = dot(ids, tags[...])[:1]
        blocks, tops, owner = [], [], []
        for start in range(0, TOK, HD):
            blocks.append(dot_t(keys[pl.ds(start, HD), :], queries))
            tops.append(jnp.max(blocks[-1], axis=0, keepdims=True))
            owner.append(0 if start < 2 * SYS_T else 1 + (start - 2 * SYS_T) // BLOCK)
        ok = [ids == bc_ref[k].astype(F32) for k in range(2)]
        for k in range(2):
            theirs = bc_r[k].astype(F32)
            ok.append(ids == jnp.concatenate([theirs, theirs], axis=1))
        largest = tops[0]
        for top, b in zip(tops[1:], owner[1:]):
            largest = jnp.maximum(largest, jnp.where(ok[b - 1], top, LOW))
        scaled = largest * SCALE
        bounds = [scaled] + [jnp.where(one, scaled, -LOW) for one in ok]
        total = None
        for k, (scores, b) in enumerate(zip(blocks, owner)):
            weights = jnp.exp2(scores * SCALE - bounds[b]).astype(BF16)
            sums = dot(vt[:, pl.ds(k * HD, HD)], weights)
            total = sums if total is None else total + sums
        weight = total[HD : HD + 1]
        return total[:HD] * (1.0 / weight), scaled + jnp.log(weight) * LOG2E

    def send_rs(xx, numerator, lse, own=False):
        for k in range(NZ):
            rs_s[xx, k] = numerator[k * SLICE : (k + 1) * SLICE].astype(BF16)
        lse_s[xx] = lse

        def to_z(k):
            zz = ((z + FAR_FIRST[k]) & 7)
            where = device(xx, zz, c, y)
            remote(rs_s.at[xx, zz], rs_r.at[x, z], rs_ss.at[xx], rs_rs, where).start()
            remote(lse_s.at[xx], lse_r.at[x, z], lse_ss.at[xx], lse_rs, where).start()

        for k in range(NZ - 1 if own else NZ):
            to_z(k)

    own_num[...], lse_s[x] = partial(x)
    def suffix_sums(part, total):
        start = pl.multiple_of(part * CHUNK, CHUNK)
        weights = jnp.exp2(ssuf[pl.ds(start, CHUNK), :] * SCALE - m_suf * SCALE)
        weights = weights.astype(BF16).astype(F32)
        turned = pltpu.roll(weights, 1, 0).T.astype(BF16)
        for i in range(2):
            nsuf[i] += dot(turned, suf_rows[i, pl.ds(start, CHUNK), :])
        return total + jnp.sum(weights, axis=0, keepdims=True)

    l_suf = lax.fori_loop(0, 2 * SUF_T // CHUNK, suffix_sums, jnp.zeros((1, HD), F32))
    l_suf = jnp.where(valid, l_suf, 1.0)
    lse_suf = jnp.where(valid, m_suf * SCALE + jnp.log(l_suf) * LOG2E, LOW)
    even = lax.rem(iota((HD, HD), 0), 2) == 0
    suf_s[...] = jnp.where(even, nsuf[0, :, other_128], nsuf[1, :, other_128]).T / l_suf
    sufml_s[...] = lse_suf
    o_suf = jnp.where(even, nsuf[0, :, own_128], nsuf[1, :, own_128]).T / l_suf
    swaps_suf = [
        remote(suf_s, suf_r, sib_s.at[3], sib_r.at[3], sibling),
        remote(sufml_s, sufml_r, sib_s.at[4], sib_r.at[4], sibling),
    ]
    for copy in swaps_suf:
        copy.start()

    def other_x(k):
        xx = ((x + k) & 3)
        await_bytes(qg.at[xx], xq_r.at[xx])
        send_rs(xx, *partial(xx))

    loop(1, NX, other_x)

    for copy in swaps_suf:
        copy.wait_recv()
    num, lse = own_num[...], lse_s[x]
    mine = place == c
    both_o = jnp.where(mine, o_suf, pltpu.roll(suf_r[...], HD - 32, 1))
    both_l = jnp.where(
        mine, jnp.broadcast_to(lse_suf, (8, HD)), pltpu.roll(jnp.broadcast_to(sufml_r[...], (8, HD)), HD - 32, 1)
    )
    shift = ((z) & 3) * 32
    both_o, both_l = pltpu.roll(both_o, shift, 1), pltpu.roll(both_l, shift, 1)[:1]
    here = lax.div(iota((1, ROWS), 1), 32) == z
    o_two = jnp.concatenate([both_o, both_o], axis=1)
    l_two = jnp.where(here, jnp.concatenate([both_l, both_l], axis=1), LOW)
    largest = jnp.maximum(lse, l_two)
    w_one, w_two = jnp.exp2(lse - largest), jnp.exp2(l_two - largest)
    norm = 1.0 / (w_one + w_two)
    num = num * (w_one * norm) + jnp.where(here, o_two, 0.0) * (w_two * norm)
    send_rs(x, num, largest + jnp.log(w_one + w_two) * LOG2E, own=True)
    self_rs = [
        pltpu.make_async_copy(rs_s.at[x, z], rs_r.at[x, z], rs_rs),
        pltpu.make_async_copy(lse_s.at[x], lse_r.at[x, z], lse_rs),
    ]
    for copy in self_rs:
        copy.start()

    await_bytes(lse_r, lse_rs)
    lses = [lse_r[xx, zz] for xx in range(NX) for zz in range(NZ)]
    largest = lses[0]
    for one in lses[1:]:
        largest = jnp.maximum(largest, one)
    factors = [jnp.exp2(one - largest) for one in lses]
    total = factors[0]
    for one in factors[1:]:
        total = total + one
    norm = 1.0 / total
    await_bytes(rs_r, rs_rs)
    num = jnp.zeros((SLICE, ROWS), F32)
    for k in range(NX * NZ):
        num = num + rs_r[k // NZ, k % NZ].astype(F32) * factors[k]
    az[x, z] = (num * norm).astype(BF16)

    def send_a(k):
        zz = ((z + FAR_FIRST[k]) & 7)
        for d in (2, 1, 3):
            remote(az.at[x, z], az.at[x, z], az_ss, ax_rs.at[x], device(((x + d) & 3), zz, c, y)).start()

        if k < NZ - 1:
            remote(az.at[x, z], az.at[x, z], az_ss, ax_rs.at[x], device(x, zz, c, y)).start()

    for k in range(NZ):
        send_a(k)
    await_bytes(az.at[x, pl.ds(0, NZ - 1)], ax_rs.at[x])
    copy_wt.wait()
    swaps[3].wait_recv()

    def finish(xx):
        ax[...] = dot_t(pick[...], az.at[xx].reshape(HD, ROWS)[...]).astype(BF16)
        attention = jnp.concatenate([ax[pl.ds(j * 32, 32), :] for j in range(GROUP)], axis=1)
        projected = dot_t(attention, wt[...])
        ys[xx, 0] = projected[:, :WIDE]
        ys[xx, 1] = projected[:, WIDE:]

        @pl.when(xx == y)
        def _():
            pltpu.make_async_copy(ys.at[xx, 0], out_ref.at[y, c], y_rs).start()

        @pl.when(xx != y)
        def _():
            remote(ys.at[xx, 0], out_ref.at[y, c], y_ss, y_rs, device(x, z, c, xx)).start()

        remote(ys.at[xx, 1], out_ref.at[y, c], y_ss, y_rs, device(x, z, o, xx)).start()

    def finish_all(k):
        far = jnp.where(k == 1, 2, jnp.where(k == 2, 1, jnp.where(k == 3, 3, 0)))
        xx = jnp.where(k == 0, x, ((y + far) & 3))

        @pl.when((k > 0) & (xx != x))
        def _():
            await_bytes(az.at[xx], ax_rs.at[xx])

        @pl.when((k == 0) | (xx != x))
        def _():
            finish(xx)

    loop(0, NX + 1, finish_all)
    await_bytes(out_ref, y_rs)

    for copy in (*swaps, *swaps_suf):
        copy.wait_send()
    await_bytes(qg.at[x, pl.ds(0, 15)], zq_s)
    await_bytes(qg.at[pl.ds(0, 3)], xq_s)
    for d in range(1, NX):
        xx = ((x + d) & 3)
        await_bytes(rs_s.at[xx], rs_ss.at[xx])
        await_bytes(lse_r.at[xx], lse_ss.at[xx])
    await_bytes(rs_s.at[x, pl.ds(0, NZ - 1)], rs_ss.at[x])
    await_bytes(lse_r.at[x, pl.ds(0, NZ - 1)], lse_ss.at[x])
    await_bytes(az.at[pl.ds(0, 3)], az_ss)
    await_bytes(az.at[x, pl.ds(0, NZ - 1)], az_ss)
    await_bytes(ys.at[pl.ds(0, 3)], y_ss)
    await_bytes(ys.at[3, 0], y_ss)


def local(queries, sys_cache, ctx_cache, block_context, context_id, suffix_cache, suffix_lengths, out_weight):
    split = queries.reshape(2, 16, HD).transpose(1, 0, 2)
    anywhere = pl.BlockSpec(memory_space=pl.ANY)
    dma = pltpu.SemaphoreType.DMA
    parts = pl.pallas_call(
        kernel,
        out_shape=jax.ShapeDtypeStruct((NY, NC, 128 // NY, WIDE), F32),
        in_specs=[anywhere] * 8,
        out_specs=anywhere,
        scratch_shapes=[
            pltpu.SMEM((2,), jnp.int32),
            pltpu.SMEM((2,), jnp.int32),
            pltpu.SMEM((2,), jnp.int32),
            pltpu.VMEM((2, GROUP + 1, 2, HD), BF16),
            pltpu.VMEM((NX, SLOTS, GROUP + 1, 2, HD), BF16),
            pltpu.VMEM((TOK, 2, HD), BF16),
            pltpu.VMEM((TOK, HD), BF16),
            pltpu.VMEM((VROWS, TOK), BF16),
            pltpu.VMEM((2, SUF_T, 2, 2 * HD), BF16),
            pltpu.VMEM((HD // 2, 2, 2 * HD), BF16),
            pltpu.VMEM((2 * SUF_T, HD), F32),
            pltpu.VMEM((2, HD, 2 * HD), F32),
            pltpu.VMEM((HD, ROWS), F32),
            pltpu.VMEM((HD, HD), F32),
            pltpu.VMEM((1, HD), F32),
            pltpu.VMEM((HD, HD), F32),
            pltpu.VMEM((1, HD), F32),
            pltpu.VMEM((2, 1, HD), jnp.int32),
            pltpu.VMEM((2, 1, HD), jnp.int32),
            pltpu.VMEM((256, 256), BF16),
            pltpu.VMEM((HD, HD), BF16),
            pltpu.VMEM((256, 256), BF16),
            pltpu.VMEM((SLOTS * 18, ROWS), BF16),
            pltpu.VMEM((NX, NZ, SLICE, ROWS), BF16),
            pltpu.VMEM((NX, 1, ROWS), F32),
            pltpu.VMEM((NX, NZ, SLICE, ROWS), BF16),
            pltpu.VMEM((NX, NZ, 1, ROWS), F32),
            pltpu.VMEM((NX, NZ, SLICE, ROWS), BF16),
            pltpu.VMEM((ROWS, HD), BF16),
            pltpu.VMEM((NC * WIDE, GROUP * HD), BF16),
            pltpu.VMEM((NX, NC, 32, WIDE), F32),
            dma((4,)),
            dma((5,)),
            dma((6,)), dma((6,)),
            dma, dma((NZ,)),
            dma, dma((NX,)),
            dma((NX,)), dma,
            dma((NX,)), dma,
            dma, dma((NX,)),
            dma, dma,
        ],
        compiler_params=pltpu.CompilerParams(
            collective_id=0, has_side_effects=True, vmem_limit_bytes=63 * 1024 * 1024
        ),
        cost_estimate=pl.CostEstimate(flops=2 * 10**9, bytes_accessed=4 * 10**6, transcendentals=2 * 10**6),
    )(
        context_id, suffix_lengths, block_context, split, sys_cache, ctx_cache, suffix_cache, out_weight.T,
    )
    return parts[..., :COLS].sum((0, 1))


def solution(mesh):
    return jax.shard_map(
        local,
        mesh=mesh,
        in_specs=(
            P("seq", "head"),
            P("seq", None, "head"),
            P("seq", None, "head"),
            P("seq"),
            P("seq"),
            P("seq", None, None, "head"),
            P("seq"),
            P("head", "seq"),
        ),
        out_specs=P("head", "seq"),
        check_vma=False,
    )
```

```python
import math

import jax
import jax.numpy as jnp
from jax import lax
from jax.experimental import pallas as pl
from jax.experimental.pallas import tpu as pltpu
from jax.sharding import PartitionSpec as P

HD = 128
NX, NZ, NC, NY = 4, 8, 2, 4
SLOTS = NZ * NC
GROUP = 8
ROWS = SLOTS * GROUP * 2
SYS_T, CTX_T, SUF_T = 64, 512, 1024
TOK = 2 * (SYS_T + CTX_T)
BLOCK = 256
COLS, WIDE = 80, 128
VROWS = HD + 16
SLICE = HD // NZ
LOG2E = math.log2(math.e)
SCALE = LOG2E / math.sqrt(HD)
LOW = -1e30
MASKED = -3e38
MESH = pl.DeviceIdType.MESH
F32, BF16 = jnp.float32, jnp.bfloat16
CHUNK = 512


def dot(a, b):
    return lax.dot_general(a, b, (((1,), (0,)), ((), ())), preferred_element_type=F32)


def dot_t(a, b):
    return lax.dot_general(a, b, (((1,), (1,)), ((), ())), preferred_element_type=F32)


def iota(shape, dim):
    return lax.broadcasted_iota(jnp.int32, shape, dim)


FAR_FIRST = (4, 5, 3, 6, 2, 7, 1, 0)
NEAR_FIRST = (0, 1, 7, 2, 6, 3, 5, 4)


def kernel(
    cid_hbm, len_hbm, bc_hbm, q_hbm, sys_hbm, ctx_hbm, suf_hbm, wt_hbm, out_ref,
    cid_ref, len_ref, bc_ref, stage, qg, kvx, keys, vt, sufx, qbd, ssuf, nsuf, own_num, o_own, lse_own, suf_s, sufml_s, suf_r, sufml_r, bc_s, bc_r,
    perm, eye, pick, tags, rs_s, lse_s, rs_r, lse_r, az, ax, wt, ys,
    loc, small, sib_s, sib_r, zq_s, zq_r, xq_s, xq_r, rs_ss, rs_rs, lse_ss, lse_rs, az_ss, ax_rs, y_ss, y_rs,
):
    seq, y = lax.axis_index("seq"), lax.axis_index("head")
    x, z, c = ((seq) >> 4), lax.rem(((seq) >> 1), NZ), ((seq) & 1)
    o = 1 - c
    slot = z * NC + c

    def device(xx, zz, cc, yy):
        return ((xx * NZ + zz) * NC + cc, yy)

    def remote(src, dst, send, recv, where):
        return pltpu.make_async_remote_copy(
            src_ref=src, dst_ref=dst, send_sem=send, recv_sem=recv, device_id=where, device_id_type=MESH
        )

    def await_bytes(ref, sem):
        pltpu.make_async_copy(ref, ref, sem).wait()

    def loop(start, stop, body):
        def step(k, _):
            body(k)
            return 0

        lax.fori_loop(start, stop, step, 0)

    sibling = device(x, z, o, y)

    barrier = pltpu.get_barrier_semaphore()

    def greet(where):
        pl.semaphore_signal(barrier, inc=1, device_id=where, device_id_type=MESH)

    def greet_z(k):
        zz = ((z + FAR_FIRST[k]) & 7)
        greet(device(x, zz, c, y))
        greet(device(x, zz, o, y))

    for k in range(NZ - 1):
        greet_z(k)
    greet(sibling)
    for d in (2, 1, 3):
        greet(device(((x + d) & 3), z, c, y))
        for cc in range(NC):
            greet(device(x, z, cc, ((y + d) & 3)))
    partners = 2 * NZ - 1 + 3 + 6

    own_128 = pl.ds(pl.multiple_of(c * HD, HD), HD)
    other_128 = pl.ds(pl.multiple_of(o * HD, HD), HD)
    own_w = pl.ds(pl.multiple_of(c * GROUP * HD, HD), GROUP * HD)
    other_w = pl.ds(pl.multiple_of(o * GROUP * HD, HD), GROUP * HD)
    copy_len = pltpu.make_async_copy(len_hbm, len_ref, small.at[0])
    copy_cid = pltpu.make_async_copy(cid_hbm, cid_ref, small.at[1])
    copy_bc = pltpu.make_async_copy(bc_hbm, bc_ref, small.at[2])
    copy_q = [
        pltpu.make_async_copy(q_hbm.at[pl.ds(g * GROUP, GROUP)], stage.at[g, pl.ds(0, GROUP)], small.at[3 + g])
        for g in range(2)
    ]
    copy_suf = pltpu.make_async_copy(suf_hbm, sufx, loc.at[0])
    copy_ctx = pltpu.make_async_copy(ctx_hbm.at[:, :, own_128], kvx.at[pl.ds(2 * SYS_T, CTX_T)], loc.at[1])
    copy_sys = pltpu.make_async_copy(sys_hbm.at[:, :, own_128], kvx.at[pl.ds(0, SYS_T)], loc.at[2])
    copy_wt = pltpu.make_async_copy(wt_hbm.at[:, own_w], wt.at[pl.ds(0, COLS)], loc.at[3])
    for copy in (copy_len, copy_cid, copy_bc, *copy_q, copy_suf, copy_ctx, copy_sys, copy_wt):
        copy.start()

    qbd[...] = jnp.zeros((HD // 2, 2, 2 * HD), BF16)
    lane = iota((1, HD), 1)
    for copy in (copy_cid, copy_bc, copy_len, *copy_q):
        copy.wait()
    ids = jnp.where(iota((2, HD), 0) == 0, cid_ref[0], cid_ref[1]).astype(F32).astype(BF16)
    stage[0, GROUP] = ids
    stage[1, GROUP] = ids
    bc_s[0] = jnp.full((1, HD), bc_ref[0], jnp.int32)
    bc_s[1] = jnp.full((1, HD), bc_ref[1], jnp.int32)
    qbd[pl.ds(c * GROUP, GROUP), :, own_128] = stage[c, pl.ds(0, GROUP)]
    qbd[pl.ds(16 + c * GROUP, GROUP), :, other_128] = stage[o, pl.ds(0, GROUP)]
    first = ((lane) & 1) == 0
    place = ((lane) >> 4)
    valid = (place == c) | (place == 2 + c)
    live = jnp.where(valid, jnp.where(first, 2 * len_ref[0], 2 * len_ref[1]), 0)
    suf_rows = sufx.reshape(2, 2 * SUF_T, 2 * HD)
    spread = qbd.reshape(HD, 2 * HD)

    def suffix_scores(part, top):
        start = pl.multiple_of(part * CHUNK, CHUNK)
        one = dot_t(suf_rows[0, pl.ds(start, CHUNK), :], spread[...])
        two = dot_t(suf_rows[1, pl.ds(start, CHUNK), :], spread[...])
        at = iota((CHUNK, HD), 0)
        at = jnp.where(((at) & 1) == 0, at + start, 1 << 20)
        scores = jnp.where(at < live, jnp.where(first, one, two), MASKED)
        ssuf[pl.ds(start, CHUNK), :] = scores
        return jnp.maximum(top, jnp.max(scores, axis=0, keepdims=True))

    flat = kvx.reshape(2 * TOK, HD)

    def take_apart(part):
        pairs = flat[pl.ds(pl.multiple_of(part * 256, 256), 256), :]
        both = dot(perm[...], pairs).astype(BF16)
        start = pl.multiple_of(part * HD, HD)
        keys[pl.ds(start, HD), :] = both[:HD]
        vt[pl.ds(0, HD), pl.ds(start, HD)] = dot_t(eye[...], both[HD:]).astype(BF16)

    pl.semaphore_wait(barrier, partners)
    copy_self = pltpu.make_async_copy(stage.at[c], qg.at[x, slot], zq_r.at[z])
    copy_self.start()

    def send_q(zz, cc):
        remote(stage.at[cc], qg.at[x, slot], zq_s, zq_r.at[z], device(x, zz, cc, y)).start()

    send_q(z, o)

    def send_z(k):
        zz = ((z + FAR_FIRST[k]) & 7)
        for cc in range(NC):
            send_q(zz, cc)

    for k in range(NZ - 1):
        send_z(k)

    swaps = [
        remote(sys_hbm.at[:, :, other_128], kvx.at[pl.ds(SYS_T, SYS_T)], sib_s.at[0], sib_r.at[0], sibling),
        remote(
            ctx_hbm.at[:, :, other_128], kvx.at[pl.ds(2 * SYS_T + CTX_T, CTX_T)], sib_s.at[1], sib_r.at[1], sibling
        ),
        remote(bc_s, bc_r, sib_s.at[2], sib_r.at[2], sibling),
        remote(wt_hbm.at[:, other_w], wt.at[pl.ds(WIDE, COLS)], sib_s.at[5], sib_r.at[5], sibling),
    ]
    for copy in swaps:
        copy.start()

    row, col = iota((256, 1), 0), iota((256, 256), 1)
    perm[...] = (col == jnp.where(row < HD, 2 * row, 2 * (row - HD) + 1)).astype(F32).astype(BF16)
    rest = row & 31
    pick[...] = (col == ((rest >> 1) << 4) + ((row >> 5) << 1) + (rest & 1)).astype(F32).astype(BF16)
    to = iota((1, ROWS), 1)
    tags[...] = (iota((SLOTS * 18, ROWS), 0) == (to >> 4) * 18 + 16 + (to & 1)).astype(F32).astype(BF16)
    eye[...] = (iota((HD, HD), 0) == iota((HD, HD), 1)).astype(F32).astype(BF16)
    vt[pl.ds(HD, 16), :] = jnp.ones((16, TOK), BF16)
    nsuf[...] = jnp.zeros((2, HD, 2 * HD), F32)
    for k in range(NC):
        wt[pl.ds(k * WIDE + COLS, WIDE - COLS), :] = jnp.zeros((WIDE - COLS, GROUP * HD), BF16)

    def pass_q(k):
        zz = ((z + NEAR_FIRST[k]) & 7)
        pairs = qg.at[x, pl.ds(zz * NC, NC)]
        await_bytes(pairs, zq_r.at[zz])
        for d in (2, 1, 3):
            remote(pairs, pairs, xq_s, xq_r.at[x], device(((x + d) & 3), z, c, y)).start()

    copy_ctx.wait()
    loop(1, 5, take_apart)
    copy_suf.wait()
    steps = 2 * SUF_T // CHUNK
    m_suf = jnp.full((1, HD), LOW, F32)
    for k in range(0, 1):
        pass_q(k)
    m_suf = lax.fori_loop(0, steps // 2, suffix_scores, m_suf)
    for k in range(1, 3):
        pass_q(k)
    m_suf = lax.fori_loop(steps // 2, 3 * steps // 4, suffix_scores, m_suf)
    for k in range(3, 5):
        pass_q(k)
    m_suf = lax.fori_loop(3 * steps // 4, steps, suffix_scores, m_suf)
    for k in range(5, 7):
        pass_q(k)
    copy_sys.wait()
    swaps[0].wait_recv()
    swaps[1].wait_recv()
    take_apart(0)
    loop(5, 9, take_apart)
    for k in range(7, 8):
        pass_q(k)
    swaps[2].wait_recv()

    def partial(xx):
        queries = jnp.concatenate(
            [qg.at[xx, k, pl.ds(0, GROUP)].reshape(16, HD)[...] for k in range(SLOTS)], axis=0
        )
        pickers = (iota((16, HD), 1) == 0).astype(F32).astype(BF16)
        ids = dot_t(pickers, qg.at[xx].reshape(SLOTS * 18, HD)[...]).astype(BF16)
        ids = dot(ids, tags[...])[:1]
        blocks, tops, owner = [], [], []
        for start in range(0, TOK, HD):
            blocks.append(dot_t(keys[pl.ds(start, HD), :], queries))
            tops.append(jnp.max(blocks[-1], axis=0, keepdims=True))
            owner.append(0 if start < 2 * SYS_T else 1 + (start - 2 * SYS_T) // BLOCK)
        ok = [ids == bc_ref[k].astype(F32) for k in range(2)]
        for k in range(2):
            theirs = bc_r[k].astype(F32)
            ok.append(ids == jnp.concatenate([theirs, theirs], axis=1))
        largest = tops[0]
        for top, b in zip(tops[1:], owner[1:]):
            largest = jnp.maximum(largest, jnp.where(ok[b - 1], top, LOW))
        scaled = largest * SCALE
        bounds = [scaled] + [jnp.where(one, scaled, -LOW) for one in ok]
        total = None
        for k, (scores, b) in enumerate(zip(blocks, owner)):
            weights = jnp.exp2(scores * SCALE - bounds[b]).astype(BF16)
            sums = dot(vt[:, pl.ds(k * HD, HD)], weights)
            total = sums if total is None else total + sums
        weight = total[HD : HD + 1]
        return total[:HD] * (1.0 / weight), scaled + jnp.log(weight) * LOG2E

    def send_rs(xx, numerator, lse, own=False):
        for k in range(NZ):
            rs_s[xx, k] = numerator[k * SLICE : (k + 1) * SLICE].astype(BF16)
        lse_s[xx] = lse

        def to_z(k):
            zz = ((z + FAR_FIRST[k]) & 7)
            where = device(xx, zz, c, y)
            remote(rs_s.at[xx, zz], rs_r.at[x, z], rs_ss.at[xx], rs_rs, where).start()
            remote(lse_s.at[xx], lse_r.at[x, z], lse_ss.at[xx], lse_rs, where).start()

        for k in range(NZ - 1 if own else NZ):
            to_z(k)

    def suffix_sums(part, total):
        start = pl.multiple_of(part * CHUNK, CHUNK)
        weights = jnp.exp2(ssuf[pl.ds(start, CHUNK), :] * SCALE - m_suf * SCALE)
        weights = weights.astype(BF16).astype(F32)
        turned = pltpu.roll(weights, 1, 0).T.astype(BF16)
        for i in range(2):
            nsuf[i] += dot(turned, suf_rows[i, pl.ds(start, CHUNK), :])
        return total + jnp.sum(weights, axis=0, keepdims=True)

    swaps_suf = [
        remote(suf_s, suf_r, sib_s.at[3], sib_r.at[3], sibling),
        remote(sufml_s, sufml_r, sib_s.at[4], sib_r.at[4], sibling),
    ]

    def rows_of(k):
        xx = (x + k) & 3

        @pl.when(k > 0)
        def _():
            await_bytes(qg.at[xx], xq_r.at[xx])

        num, lse = partial(xx)

        @pl.when(k == 0)
        def _():
            own_num[...] = num
            lse_s[x] = lse
            l_suf = lax.fori_loop(0, 2 * SUF_T // CHUNK, suffix_sums, jnp.zeros((1, HD), F32))
            l_suf = jnp.where(valid, l_suf, 1.0)
            lse_suf = jnp.where(valid, m_suf * SCALE + jnp.log(l_suf) * LOG2E, LOW)
            even = lax.rem(iota((HD, HD), 0), 2) == 0
            suf_s[...] = jnp.where(even, nsuf[0, :, other_128], nsuf[1, :, other_128]).T / l_suf
            sufml_s[...] = lse_suf
            lse_own[...] = lse_suf
            o_own[...] = jnp.where(even, nsuf[0, :, own_128], nsuf[1, :, own_128]).T / l_suf
            for copy in swaps_suf:
                copy.start()

        @pl.when(k > 0)
        def _():
            send_rs(xx, num, lse)

    loop(0, NX, rows_of)

    for copy in swaps_suf:
        copy.wait_recv()
    num, lse, o_suf, lse_suf = own_num[...], lse_s[x], o_own[...], lse_own[...]
    mine = place == c
    both_o = jnp.where(mine, o_suf, pltpu.roll(suf_r[...], HD - 32, 1))
    both_l = jnp.where(
        mine, jnp.broadcast_to(lse_suf, (8, HD)), pltpu.roll(jnp.broadcast_to(sufml_r[...], (8, HD)), HD - 32, 1)
    )
    shift = ((z) & 3) * 32
    both_o, both_l = pltpu.roll(both_o, shift, 1), pltpu.roll(both_l, shift, 1)[:1]
    here = lax.div(iota((1, ROWS), 1), 32) == z
    o_two = jnp.concatenate([both_o, both_o], axis=1)
    l_two = jnp.where(here, jnp.concatenate([both_l, both_l], axis=1), LOW)
    largest = jnp.maximum(lse, l_two)
    w_one, w_two = jnp.exp2(lse - largest), jnp.exp2(l_two - largest)
    norm = 1.0 / (w_one + w_two)
    num = num * (w_one * norm) + jnp.where(here, o_two, 0.0) * (w_two * norm)
    send_rs(x, num, largest + jnp.log(w_one + w_two) * LOG2E, own=True)
    self_rs = [
        pltpu.make_async_copy(rs_s.at[x, z], rs_r.at[x, z], rs_rs),
        pltpu.make_async_copy(lse_s.at[x], lse_r.at[x, z], lse_rs),
    ]
    for copy in self_rs:
        copy.start()

    await_bytes(lse_r, lse_rs)
    lses = [lse_r[xx, zz] for xx in range(NX) for zz in range(NZ)]
    largest = lses[0]
    for one in lses[1:]:
        largest = jnp.maximum(largest, one)
    factors = [jnp.exp2(one - largest) for one in lses]
    total = factors[0]
    for one in factors[1:]:
        total = total + one
    norm = 1.0 / total
    await_bytes(rs_r, rs_rs)
    num = jnp.zeros((SLICE, ROWS), F32)
    for k in range(NX * NZ):
        num = num + rs_r[k // NZ, k % NZ].astype(F32) * factors[k]
    az[x, z] = (num * norm).astype(BF16)

    def send_a(k):
        zz = ((z + FAR_FIRST[k]) & 7)
        for d in (2, 1, 3):
            remote(az.at[x, z], az.at[x, z], az_ss, ax_rs.at[x], device(((x + d) & 3), zz, c, y)).start()

        if k < NZ - 1:
            remote(az.at[x, z], az.at[x, z], az_ss, ax_rs.at[x], device(x, zz, c, y)).start()

    for k in range(NZ):
        send_a(k)
    await_bytes(az.at[x, pl.ds(0, NZ - 1)], ax_rs.at[x])
    copy_wt.wait()
    swaps[3].wait_recv()

    def finish(xx):
        ax[...] = dot_t(pick[...], az.at[xx].reshape(HD, ROWS)[...]).astype(BF16)
        attention = jnp.concatenate([ax[pl.ds(j * 32, 32), :] for j in range(GROUP)], axis=1)
        projected = dot_t(attention, wt[...])
        ys[xx, 0] = projected[:, :WIDE]
        ys[xx, 1] = projected[:, WIDE:]

        @pl.when(xx == y)
        def _():
            pltpu.make_async_copy(ys.at[xx, 0], out_ref.at[y, c], y_rs).start()

        @pl.when(xx != y)
        def _():
            remote(ys.at[xx, 0], out_ref.at[y, c], y_ss, y_rs, device(x, z, c, xx)).start()

        remote(ys.at[xx, 1], out_ref.at[y, c], y_ss, y_rs, device(x, z, o, xx)).start()

    def finish_all(k):
        far = jnp.where(k == 1, 2, jnp.where(k == 2, 1, jnp.where(k == 3, 3, 0)))
        xx = jnp.where(k == 0, x, ((y + far) & 3))

        @pl.when((k > 0) & (xx != x))
        def _():
            await_bytes(az.at[xx], ax_rs.at[xx])

        @pl.when((k == 0) | (xx != x))
        def _():
            finish(xx)

    loop(0, NX + 1, finish_all)
    await_bytes(out_ref, y_rs)

    for copy in (*swaps, *swaps_suf):
        copy.wait_send()
    await_bytes(qg.at[x, pl.ds(0, 15)], zq_s)
    await_bytes(qg.at[pl.ds(0, 3)], xq_s)
    for d in range(1, NX):
        xx = ((x + d) & 3)
        await_bytes(rs_s.at[xx], rs_ss.at[xx])
        await_bytes(lse_r.at[xx], lse_ss.at[xx])
    await_bytes(rs_s.at[x, pl.ds(0, NZ - 1)], rs_ss.at[x])
    await_bytes(lse_r.at[x, pl.ds(0, NZ - 1)], lse_ss.at[x])
    await_bytes(az.at[pl.ds(0, 3)], az_ss)
    await_bytes(az.at[x, pl.ds(0, NZ - 1)], az_ss)
    await_bytes(ys.at[pl.ds(0, 3)], y_ss)
    await_bytes(ys.at[3, 0], y_ss)


def local(queries, sys_cache, ctx_cache, block_context, context_id, suffix_cache, suffix_lengths, out_weight):
    split = queries.reshape(2, 16, HD).transpose(1, 0, 2)
    anywhere = pl.BlockSpec(memory_space=pl.ANY)
    dma = pltpu.SemaphoreType.DMA
    parts = pl.pallas_call(
        kernel,
        out_shape=jax.ShapeDtypeStruct((NY, NC, 128 // NY, WIDE), F32),
        in_specs=[anywhere] * 8,
        out_specs=anywhere,
        scratch_shapes=[
            pltpu.SMEM((2,), jnp.int32),
            pltpu.SMEM((2,), jnp.int32),
            pltpu.SMEM((2,), jnp.int32),
            pltpu.VMEM((2, GROUP + 1, 2, HD), BF16),
            pltpu.VMEM((NX, SLOTS, GROUP + 1, 2, HD), BF16),
            pltpu.VMEM((TOK, 2, HD), BF16),
            pltpu.VMEM((TOK, HD), BF16),
            pltpu.VMEM((VROWS, TOK), BF16),
            pltpu.VMEM((2, SUF_T, 2, 2 * HD), BF16),
            pltpu.VMEM((HD // 2, 2, 2 * HD), BF16),
            pltpu.VMEM((2 * SUF_T, HD), F32),
            pltpu.VMEM((2, HD, 2 * HD), F32),
            pltpu.VMEM((HD, ROWS), F32),
            pltpu.VMEM((HD, HD), F32),
            pltpu.VMEM((1, HD), F32),
            pltpu.VMEM((HD, HD), F32),
            pltpu.VMEM((1, HD), F32),
            pltpu.VMEM((HD, HD), F32),
            pltpu.VMEM((1, HD), F32),
            pltpu.VMEM((2, 1, HD), jnp.int32),
            pltpu.VMEM((2, 1, HD), jnp.int32),
            pltpu.VMEM((256, 256), BF16),
            pltpu.VMEM((HD, HD), BF16),
            pltpu.VMEM((256, 256), BF16),
            pltpu.VMEM((SLOTS * 18, ROWS), BF16),
            pltpu.VMEM((NX, NZ, SLICE, ROWS), BF16),
            pltpu.VMEM((NX, 1, ROWS), F32),
            pltpu.VMEM((NX, NZ, SLICE, ROWS), BF16),
            pltpu.VMEM((NX, NZ, 1, ROWS), F32),
            pltpu.VMEM((NX, NZ, SLICE, ROWS), BF16),
            pltpu.VMEM((ROWS, HD), BF16),
            pltpu.VMEM((NC * WIDE, GROUP * HD), BF16),
            pltpu.VMEM((NX, NC, 32, WIDE), F32),
            dma((4,)),
            dma((5,)),
            dma((6,)), dma((6,)),
            dma, dma((NZ,)),
            dma, dma((NX,)),
            dma((NX,)), dma,
            dma((NX,)), dma,
            dma, dma((NX,)),
            dma, dma,
        ],
        compiler_params=pltpu.CompilerParams(
            collective_id=0, has_side_effects=True, vmem_limit_bytes=63 * 1024 * 1024
        ),
        cost_estimate=pl.CostEstimate(flops=2 * 10**9, bytes_accessed=4 * 10**6, transcendentals=2 * 10**6),
    )(
        context_id, suffix_lengths, block_context, split, sys_cache, ctx_cache, suffix_cache, out_weight.T,
    )
    return parts[..., :COLS].sum((0, 1))


def solution(mesh):
    return jax.shard_map(
        local,
        mesh=mesh,
        in_specs=(
            P("seq", "head"),
            P("seq", None, "head"),
            P("seq", None, "head"),
            P("seq"),
            P("seq"),
            P("seq", None, None, "head"),
            P("seq"),
            P("head", "seq"),
        ),
        out_specs=P("head", "seq"),
        check_vma=False,
    )
```
